128 devices in a mesh: ocn: 32 (over y, x, core), col: 4 (over z).
Axes of the slice: x: 4, y: 4, z: 4, core: 2. Of those that a mesh axis runs over, the one named last changes fastest.
Arguments:
- air_flux: float32 [8, 262144], P(None, ('ocn', 'col')), may hold values from -6 to 6
- send_index: int32 [128, 128, 16], P(('ocn', 'col')), may hold values from 0 to 2047
- remap_column: int32 [4, 262144], P(None, ('ocn', 'col')), may hold values from 0 to 2047
- remap_weight: float32 [4, 262144], P(None, ('ocn', 'col')), may hold values from 0.05 to 0.5
- halo_send: int32 [128, 4, 128], P(('ocn', 'col')), may hold values from 0 to 2047
- neighbours: int32 [6, 262144], P(None, ('ocn', 'col')), may hold values from 0 to 2559
- gradient_weight: float32 [2, 6, 262144], P(None, None, ('ocn', 'col')), may hold values from -0.36 to 0.36
- coriolis: float32 [262144], P(('ocn', 'col')), may hold values from -0.25 to 0.25
- sea_surface: float32 [262144], P(('ocn', 'col')), may hold values from -3 to 3
- velocity: float32 [2, 262144], P(None, ('ocn', 'col')), may hold values from -3 to 3
- lateral_weight: float32 [6, 262144], P(None, ('ocn', 'col')), may hold values from 0.005 to 0.08
- layer_count: int32 [262144], P(('ocn', 'col')), may hold values from 16 to 64
- thickness: float32 [64, 262144], P(None, ('ocn', 'col')), may hold values from 2 to 12
- diffusivity: float32 [63, 262144], P(None, ('ocn', 'col')), may hold values from 0.02 to 20
- tracers: float32 [4, 64, 262144], P(None, None, ('ocn', 'col')), may hold values from -6 to 6
Outputs:
- mixed_tracers: float32 [4, 64, 262144], P(None, None, ('ocn', 'col'))
- final_surface: float32 [262144], P(('ocn', 'col'))
- final_velocity: float32 [2, 262144], P(None, ('ocn', 'col'))
The draws below stay inside these ranges and needn't reach their ends.
Inputs may be any that keep to these rules, and one draw needn't show every extreme that they name: `send_index`: entry [q, r, j] is one of device q's own 2048 atmosphere cells, counted from its first. `halo_send`: entries are cells of the sending partition, counted from its first. `neighbours`: values under 2048 are the partition's own cells; the rest are halo blocks of 128 in the order of partners at offsets 1, -1, 2, -2.
All inputs are finite; a program needn't handle non-finite values.
Results may differ from the reference program's by a relative error of at most 0.00002.
Values sent between devices are 32-bit elements; how exact they have to be, the bound alone decides.
A program may use at most 128 MiB of HBM per device.

```python
import math
import jax
import jax.numpy as jnp

FIELDS = 8
TRACER_COUNT = 4
INTERSECTION = 4
EDGES = 6
SUBCYCLES = 8
LAYERS = 64
ATM_DEV = 2048
CELLS_DEV = 2048
HALO = 128
SLOTS = 16
RECV_DEV = 2048
NCELLS = 262144
ATM_CELLS = 262144
N_OCN = 32
N_COL = 4
DEVICES = 128


def plant(values, rng, least, top_value):
    place = [jax.random.randint(jax.random.fold_in(rng, axis), (), 0, length) for axis, length in enumerate(values.shape)]
    widest = values.shape.index(max(values.shape))
    next_to = place[:widest] + [(place[widest] + 1) % values.shape[widest]] + place[widest + 1:]
    return values.at[tuple(place)].set(least).at[tuple(next_to)].set(top_value)


def level_of(key, shape, pieces, smallest, high):
    level = 1.0
    for position, parts in pieces:
        steps = jax.random.uniform(jax.random.fold_in(jax.random.fold_in(key, 6), position), (parts,), jnp.float32, smallest / len(pieces), high / len(pieces))
        level = level * jnp.repeat(jnp.exp(steps), shape[position] // parts).reshape((-1,) + (1,) * (len(shape) - 1 - position))
    return level


def scatter_about(own_key, dims, scale, bound, shards=(), held_as=jnp.bfloat16):
    entries = jax.random.normal(own_key, dims, jnp.float32) * scale
    if len(shards) > 0:
        entries = level_of(own_key, dims, shards, -0.22, 0.18) * entries
    return jnp.clip(entries, min=-bound, max=bound).astype(held_as)


def setup_inputs(seed: int = 0) -> dict:
    seeds = jax.random.split(jax.random.key(seed), 16)
    air_flux = scatter_about(seeds[0], (FIELDS, ATM_CELLS), 1.0, 6.0, ((1, 128),), jnp.float32)
    send_index = plant(jax.random.randint(seeds[1], (DEVICES, DEVICES, SLOTS), 0, ATM_DEV), jax.random.fold_in(seeds[1], 1), 0, ATM_DEV - 1).astype(jnp.int32)
    remap_column = plant(jax.random.randint(seeds[2], (INTERSECTION, NCELLS), 0, RECV_DEV), jax.random.fold_in(seeds[2], 1), 0, RECV_DEV - 1).astype(jnp.int32)
    remap_weight = jnp.clip(0.05 + 0.45 * jax.random.uniform(seeds[3], (INTERSECTION, NCELLS), jnp.float32) ** level_of(seeds[3], (INTERSECTION, NCELLS), ((1, 128),), -0.2, 0.2), 0.05, 0.5)
    halo_send = plant(jax.random.randint(seeds[4], (DEVICES, 4, HALO), 0, CELLS_DEV), jax.random.fold_in(seeds[4], 1), 0, CELLS_DEV - 1).astype(jnp.int32)
    neighbours = plant(jax.random.randint(seeds[5], (EDGES, NCELLS), 0, CELLS_DEV + 4 * HALO), jax.random.fold_in(seeds[5], 1), 0, (CELLS_DEV + 4 * HALO) - 1).astype(jnp.int32)
    gradient_weight = scatter_about(seeds[6], (2, EDGES, NCELLS), 0.06, 0.36, ((2, 128),), jnp.float32)
    coriolis = jnp.clip(jax.random.uniform(seeds[7], (NCELLS,), jnp.float32, -0.25, 0.25) * level_of(seeds[7], (NCELLS,), ((0, 128),), -0.4, 0.0), -0.25, 0.25)
    sea_surface = scatter_about(seeds[8], (NCELLS,), 0.5, 3.0, ((0, 128),), jnp.float32)
    velocity = scatter_about(seeds[9], (2, NCELLS), 0.5, 3.0, ((1, 128),), jnp.float32)
    lateral_weight = jnp.clip(jnp.exp(math.log(0.08) - 2.7725887 * jax.random.uniform(seeds[10], (EDGES, NCELLS), jnp.float32) ** level_of(seeds[10], (EDGES, NCELLS), ((1, 128),), -0.2, 0.2)), 0.005, 0.08)
    layer_count = plant(jax.random.randint(seeds[11], (NCELLS,), LAYERS // 4, LAYERS + 1), jax.random.fold_in(seeds[11], 1), LAYERS // 4, LAYERS).astype(jnp.int32)
    thickness = jnp.clip(jnp.exp(math.log(12.0) - 1.7917595 * jax.random.uniform(seeds[12], (LAYERS, NCELLS), jnp.float32) ** level_of(seeds[12], (LAYERS, NCELLS), ((1, 128),), -0.2, 0.2)), 2.0, 12.0)
    diffusivity = jnp.clip(jnp.exp(math.log(20.0) - 6.9077553 * jax.random.uniform(seeds[13], (LAYERS - 1, NCELLS), jnp.float32) ** level_of(seeds[13], (LAYERS - 1, NCELLS), ((1, 128),), -0.2, 0.2)), 0.02, 20.0)
    tracers = scatter_about(seeds[14], (TRACER_COUNT, LAYERS, NCELLS), 1.0, 6.0, ((2, 128),), jnp.float32)
    return dict(air_flux=air_flux, send_index=send_index, remap_column=remap_column, remap_weight=remap_weight, halo_send=halo_send, neighbours=neighbours, gradient_weight=gradient_weight, coriolis=coriolis, sea_surface=sea_surface, velocity=velocity, lateral_weight=lateral_weight, layer_count=layer_count, thickness=thickness, diffusivity=diffusivity, tracers=tracers)


cycle_offsets = (1, -1, 2, -2)
flux_gain = 2.0
force_gain = 0.05


def difference_sum(source, centre, neighbour_index, weights):
    accumulated = weights[0] * (jnp.take(source, neighbour_index[0], axis=-1) - centre)
    for slot_index in range(1, neighbour_index.shape[0]):
        accumulated = accumulated + weights[slot_index] * (jnp.take(source, neighbour_index[slot_index], axis=-1) - centre)
    return accumulated


def vertical_mix(values, thickness, top_thickness, diffusivity, active, surface):
    levels = values.shape[1]
    thicknesses = [top_thickness] + [thickness[depth_index] for depth_index in range(1, levels)]
    couple = [diffusivity[depth_index] * 2.0 / (thicknesses[depth_index] + thicknesses[depth_index + 1]) * active[depth_index + 1] for depth_index in range(levels - 1)]
    ratios = []
    scaled = []
    for depth_index in range(levels):
        diagonal = thicknesses[depth_index]
        right_side = thicknesses[depth_index] * values[:, depth_index]
        if depth_index == 0:
            right_side = right_side + flux_gain * surface
        if depth_index > 0:
            diagonal = diagonal + couple[depth_index - 1]
        if depth_index < levels - 1:
            diagonal = diagonal + couple[depth_index]
        if depth_index > 0:
            diagonal = diagonal - couple[depth_index - 1] * ratios[depth_index - 1]
            right_side = right_side + couple[depth_index - 1] * scaled[depth_index - 1]
        if depth_index < levels - 1:
            ratios.append(couple[depth_index] / diagonal)
        else:
            ratios.append(jnp.zeros_like(diagonal))
        scaled.append(right_side / diagonal)
    solved = [None] * levels
    solved[levels - 1] = scaled[levels - 1]
    for depth_index in range(levels - 2, -1, -1):
        solved[depth_index] = scaled[depth_index] + ratios[depth_index] * solved[depth_index + 1]
    return jnp.stack(solved, axis=1)


def reference(air_flux, send_index, remap_column, remap_weight, halo_send, neighbours, gradient_weight, coriolis, sea_surface, velocity, lateral_weight, layer_count, thickness, diffusivity, tracers):
    partitions = N_OCN * N_COL
    slot_number = jnp.arange(RECV_DEV, dtype=jnp.int32)
    source_part = slot_number // SLOTS
    source_slot = slot_number % SLOTS
    receiver = jnp.arange(partitions, dtype=jnp.int32)
    air_index = source_part[None, :] * ATM_DEV + send_index[source_part[None, :], receiver[:, None], source_slot[None, :]]
    cell_number = jnp.arange(CELLS_DEV * partitions, dtype=jnp.int32)
    home_part = cell_number // CELLS_DEV
    surface_flux = jnp.zeros((air_flux.shape[0], cell_number.shape[0]), jnp.float32)
    for intersection_index in range(remap_column.shape[0]):
        source = air_index[home_part, remap_column[intersection_index]]
        surface_flux = surface_flux + remap_weight[intersection_index] * jnp.take(air_flux, source, axis=1)
    local_slot = neighbours
    halo_block = jnp.clip((local_slot - CELLS_DEV) // HALO, 0, 3).astype(jnp.int32)
    within = (jnp.clip(local_slot - CELLS_DEV, 0, 4 * HALO - 1) % HALO).astype(jnp.int32)
    shift_table = jnp.array(cycle_offsets, dtype=jnp.int32)
    partner = (home_part[None, :] + shift_table[halo_block]) % partitions
    remote = partner * CELLS_DEV + halo_send[partner, halo_block, within]
    neighbour_cell = jnp.where(local_slot < CELLS_DEV, home_part[None, :] * CELLS_DEV + local_slot, remote).astype(jnp.int32)
    weights = jnp.swapaxes(gradient_weight, 0, 1)
    elevation = sea_surface
    velocity_now = velocity
    for subcycle in range(SUBCYCLES):
        height = elevation + surface_flux[6]
        gradient = difference_sum(height, height, neighbour_cell, weights)
        turned = jnp.stack((velocity_now[1], -velocity_now[0]))
        velocity_next = velocity_now - gradient + coriolis * turned + force_gain * surface_flux[4:6]
        spread_parts = difference_sum(velocity_next, velocity_next, neighbour_cell, weights)
        elevation = elevation - (spread_parts[0] + spread_parts[1]) + force_gain * surface_flux[7]
        velocity_now = velocity_next
    active = (jnp.arange(LAYERS, dtype=jnp.int32)[:, None] < layer_count[None, :]).astype(jnp.float32)
    diffused = tracers + active * difference_sum(tracers, tracers, neighbour_cell, lateral_weight)
    mixed_tracers = vertical_mix(diffused, thickness, thickness[0] + jnp.tanh(elevation), diffusivity, active, surface_flux[0:4])
    return mixed_tracers, elevation, velocity_now
```

```python
import jax
import jax.numpy as jnp
from jax import lax
from jax.experimental import pallas as pl
from jax.experimental.pallas import tpu as pltpu
from jax.sharding import PartitionSpec as P

F32 = jnp.float32
BF16 = jnp.bfloat16
I32 = jnp.int32
MESH = pl.DeviceIdType.MESH

SUBCYCLES = 8
LAYERS = 64
TRACERS = 4
ROWS = TRACERS * LAYERS
EDGES = 6
BLOCKS = 16
OFFSETS = (1, -1, 2, -2)
DISTANCES = (1, -1, 2, -2, 3, -3, 4, -4)
SEND_ORDER = (2, 3, 4, 5, 0, 1, 6, 7)
FLUX_GAIN = 2.0
FORCE_GAIN = 0.05

NB, G0, G1, COR, FORCE, VEL, FIXED = 0, 6, 12, 18, 19, 21, 24
N_COLS = 256
K_ROWS = 512


def wide(row):
    return jnp.broadcast_to(row, (8, 128))


def lane_pick(source, lane):
    return jnp.take_along_axis(source, lane, axis=1, mode="promise_in_bounds")


def swap_groups(tile):
    sub = lax.broadcasted_iota(I32, (8, 128), 0)
    group = lax.broadcasted_iota(I32, (8, 128), 1) // 16
    apart = (group - sub) & 7
    out = tile
    for k in range(1, 8):
        moved = pltpu.roll(pltpu.roll(tile, 8 - k, 0), 16 * k, 1)
        out = jnp.where(apart == k, moved, out)
    return out


def pack_kernel(air_ref, index_ref, out_ref):
    for group in range(BLOCKS):
        index = wide(index_ref[pl.ds(group, 1), :])
        lane, block = index & 127, index >> 7
        got = jnp.zeros((8, 128), F32)
        for j in range(BLOCKS):
            got = jnp.where(block == j, lane_pick(air_ref[:, pl.ds(j * 128, 128)], lane), got)
        out_ref[pl.ds(group * 8, 8), :] = swap_groups(got)


def ocean_kernel(
    ocn_size,
    col_size,
    arrived,
    column,
    remap_weight,
    halo_send,
    neighbours,
    gradient,
    coriolis,
    surface,
    velocity,
    lateral,
    count,
    thick_hbm,
    diffusivity_hbm,
    tracer_hbm,
    mixed,
    final_surface,
    final_velocity,
    thick,
    diffus,
    tracer,
    tab,
    received,
    flux,
    list_fixed,
    ghost_fixed,
    own_lane,
    own_block,
    list_lane,
    list_block,
    list_g,
    ghost_lane,
    ghost_block,
    ghost_g,
    height,
    speed,
    ghost_rows,
    message,
    inbox,
    halo_out,
    halo_in,
    parts,
    halo_parts,
    total,
    profile,
    thick_cells,
    diffus_cells,
    gain_here,
    gain_below,
    gain_above,
    load_sem,
    fixed_send,
    fixed_recv,
    halo_send_sem,
    halo_recv,
    round_send,
    round_recv,
):
    devices = ocn_size * col_size
    me = lax.axis_index("ocn") * col_size + lax.axis_index("col")

    def device(distance):
        target = lax.rem(me + (distance + devices), devices)
        return (target // col_size, lax.rem(target, col_size))

    load_tracer = pltpu.make_async_copy(tracer_hbm, tracer, load_sem.at[0])
    load_thick = pltpu.make_async_copy(thick_hbm, thick, load_sem.at[1])
    load_diffus = pltpu.make_async_copy(diffusivity_hbm, diffus, load_sem.at[2])
    load_tracer.start()
    load_thick.start()
    load_diffus.start()

    barrier = pltpu.get_barrier_semaphore()
    for distance in DISTANCES:
        pl.semaphore_signal(barrier, inc=1, device_id=device(distance), device_id_type=MESH)

    for c in range(BLOCKS):
        cells = pl.ds(c * 128, 128)
        tab[pl.ds(NB * 16 + c, EDGES, stride=16), :] = neighbours[:, cells].astype(F32)
        tab[pl.ds(G0 * 16 + c, EDGES, stride=16), :] = gradient[0, :, cells]
        tab[pl.ds(G1 * 16 + c, EDGES, stride=16), :] = gradient[1, :, cells]
        tab[pl.ds(VEL * 16 + c, 2, stride=16), :] = velocity[:, cells]
    tab[pl.ds(COR * 16, 16), :] = coriolis[...]
    tab[pl.ds(23 * 16, 16), :] = jnp.zeros((16, 128), F32)
    for t in range(12):
        index = tab[pl.ds(t * 8, 8), :].astype(I32)
        own_lane[pl.ds(t * 8, 8), :] = index & 127
        own_block[pl.ds(t * 8, 8), :] = index >> 7

    load_tracer.wait()
    for t in range(TRACERS):
        rows = pl.ds(t * LAYERS, LAYERS)
        value = tracer[rows, :]
        high = value.astype(BF16)
        parts[rows, :] = high
        parts[pl.ds(ROWS + t * LAYERS, LAYERS), :] = (value - high.astype(F32)).astype(BF16)
    place = lax.broadcasted_iota(I32, (2048, 128), 0)
    for b in range(4):
        chosen = jnp.where(place == halo_send[pl.ds(b, 1), :], 1.0, 0.0).astype(BF16)
        both = jnp.dot(parts[...], chosen, preferred_element_type=F32)
        halo_out[b] = both[:ROWS] + both[ROWS:]
    pl.semaphore_wait(barrier, len(DISTANCES))
    for b in range(4):
        pltpu.make_async_remote_copy(
            halo_out.at[b], halo_in.at[b], halo_send_sem, halo_recv,
            device_id=device(-OFFSETS[b]), device_id_type=MESH,
        ).start()

    for r in range(BLOCKS):
        received[r] = swap_groups(arrived[pl.ds(r * 8, 8), :])

    def remap(c, carry):
        cells = pl.ds(pl.multiple_of(c * 128, 128), 128)
        result = jnp.zeros((8, 128), F32)
        for k in range(4):
            index = wide(column[pl.ds(k, 1), cells])
            lane, block = index & 127, index >> 7
            got = jnp.zeros((8, 128), F32)
            for j in range(BLOCKS):
                got = jnp.where(block == j, lane_pick(received[j], lane), got)
            result = result + wide(remap_weight[pl.ds(k, 1), cells]) * got
        flux[pl.ds(c, 8, stride=16), :] = result
        return carry

    lax.fori_loop(0, BLOCKS, remap, 0, unroll=4)
    tab[pl.ds(FORCE * 16, 32), :] = flux[pl.ds(64, 32), :]

    lists = jnp.concatenate([halo_send[...], halo_send[...]], axis=0)
    lists_lane, lists_block = lists & 127, lists >> 7

    def list_values(load):
        got = jnp.zeros((8, 128), F32)
        for j in range(BLOCKS):
            got = jnp.where(lists_block == j, lane_pick(wide(load(j)), lists_lane), got)
        return got

    def collect(field, carry):
        got = list_values(lambda j: tab[pl.ds(field * 16 + j, 1), :])
        list_fixed[pl.ds(field, 4, stride=FIXED), :] = got[:4]
        return carry

    lax.fori_loop(0, FIXED, collect, 0, unroll=4)
    for b in range(4):
        rows = pl.ds(b * FIXED, FIXED)
        pltpu.make_async_remote_copy(
            list_fixed.at[rows], ghost_fixed.at[rows], fixed_send, fixed_recv,
            device_id=device(-OFFSETS[b]), device_id_type=MESH,
        ).start()

    def by_edge(fixed, lane_ref, block_ref, g_ref):
        for b in range(4):
            index = fixed[pl.ds(b * FIXED + NB, EDGES), :].astype(I32)
            lane_ref[pl.ds(b, EDGES, stride=4), :] = index & 127
            block_ref[pl.ds(b, EDGES, stride=4), :] = index >> 7
            g_ref[pl.ds(b, EDGES, stride=4), :] = fixed[pl.ds(b * FIXED + G0, EDGES), :]
            g_ref[pl.ds(24 + b, EDGES, stride=4), :] = fixed[pl.ds(b * FIXED + G1, EDGES), :]

    by_edge(list_fixed, list_lane, list_block, list_g)

    def both_halves(tile):
        return tile + pltpu.roll(tile, 4, 0)

    def send_round(s, elevation):
        for half in range(2):
            height[pl.ds(half * 8, 8), :] = elevation[half] + flux[pl.ds(96 + half * 8, 8), :]
        centre = list_values(lambda j: height[pl.ds(j, 1), :])
        first = jnp.zeros((8, 128), F32)
        second = jnp.zeros((8, 128), F32)
        for t in range(3):
            lane, block = list_lane[pl.ds(t * 8, 8), :], list_block[pl.ds(t * 8, 8), :]
            got = centre
            for j in range(BLOCKS):
                got = jnp.where(block == j, lane_pick(wide(height[pl.ds(j, 1), :]), lane), got)
            first = first + list_g[pl.ds(t * 8, 8), :] * (got - centre)
            second = second + list_g[pl.ds(24 + t * 8, 8), :] * (got - centre)
        first, second = both_halves(first), both_halves(second)
        for b in range(4):
            message[s, b, 0:4, :] = centre[:4]
            message[s, b, 4:5, :] = first[b : b + 1]
            message[s, b, 5:6, :] = second[b : b + 1]
            message[s, b, 6:8, :] = jnp.zeros((2, 128), F32)
        for k in SEND_ORDER:
            pltpu.make_async_remote_copy(
                message.at[s, k if k < 4 else 0], inbox.at[s, k], round_send, round_recv.at[s],
                device_id=device(-DISTANCES[k]), device_id_type=MESH,
            ).start()

    def own_sum(ranges, centres):
        sums = [[jnp.zeros((8, 128), F32) for _ in range(2)] for _ in range(2)]
        for t in range(12):
            half, rows = t % 2, pl.ds(t * 8, 8)
            lane, block = own_lane[rows, :], own_block[rows, :]
            got = centres[half]
            for j in ranges:
                got = jnp.where(block == j, lane_pick(wide(height[pl.ds(j, 1), :]), lane), got)
            apart = got - centres[half]
            for axis in range(2):
                weight = tab[pl.ds((G0 + 6 * axis) * 16 + t * 8, 8), :]
                sums[axis][half] = sums[axis][half] + weight * apart
        return sums

    def take_round(s, elevation, flow, ghost_flow, partial):
        for b in range(4):
            height[pl.ds(16 + b, 1), :] = inbox[s, b, b : b + 1, :]
            for copy in range(2):
                for source in range(4):
                    distance = OFFSETS[b] + OFFSETS[source]
                    if distance == 0:
                        row = message[s, 0, source : source + 1, :]
                    else:
                        row = inbox[s, DISTANCES.index(distance), source : source + 1, :]
                    ghost_rows[pl.ds(source * 8 + copy * 4 + b, 1), :] = row
                ghost_rows[pl.ds(32 + copy * 4 + b, 1), :] = inbox[s, b, b : b + 1, :]
                ghost_rows[pl.ds(40 + copy * 4 + b, 1), :] = inbox[s, b, 4:5, :]
                ghost_rows[pl.ds(48 + copy * 4 + b, 1), :] = inbox[s, b, 5:6, :]
        centres = [height[pl.ds(half * 8, 8), :] for half in range(2)]
        rest = own_sum(range(16, 20), centres)
        centre = ghost_rows[pl.ds(32, 8), :]
        ghost_sums = [jnp.zeros((8, 128), F32) for _ in range(2)]
        for t in range(3):
            rows = pl.ds(t * 8, 8)
            lane, block = ghost_lane[rows, :], ghost_block[rows, :]
            got = centre
            for j in range(4):
                got = jnp.where(block == 16 + j, lane_pick(ghost_rows[pl.ds(j * 8, 8), :], lane), got)
            for axis in range(2):
                ghost_sums[axis] = ghost_sums[axis] + ghost_g[pl.ds(axis * 24 + t * 8, 8), :] * (got - centre)
        ghost_sums = [both_halves(ghost_sums[a]) + ghost_rows[pl.ds(40 + 8 * a, 8), :] for a in range(2)]

        turn = ghost_rows[pl.ds(56, 8), :]
        ghost_next = (
            ghost_flow[0] - ghost_sums[0] + turn * ghost_flow[1] + FORCE_GAIN * ghost_rows[pl.ds(64, 8), :],
            ghost_flow[1] - ghost_sums[1] - turn * ghost_flow[0] + FORCE_GAIN * ghost_rows[pl.ds(72, 8), :],
        )
        flow_next = []
        for half in range(2):
            turn = tab[pl.ds(COR * 16 + half * 8, 8), :]
            force = [tab[pl.ds((FORCE + a) * 16 + half * 8, 8), :] for a in range(2)]
            grad = [partial[a][half] + rest[a][half] for a in range(2)]
            flow_next.append(
                (
                    flow[half][0] - grad[0] + turn * flow[half][1] + FORCE_GAIN * force[0],
                    flow[half][1] - grad[1] - turn * flow[half][0] + FORCE_GAIN * force[1],
                )
            )
        for a in range(2):
            for half in range(2):
                speed[pl.ds(a * 24 + half * 8, 8), :] = flow_next[half][a]
            speed[pl.ds(a * 24 + 16, 8), :] = ghost_next[a]
        spread = [jnp.zeros((8, 128), F32) for _ in range(2)]
        for t in range(12):
            half, rows = t % 2, pl.ds(t * 8, 8)
            lane, block = own_lane[rows, :], own_block[rows, :]
            got = [jnp.zeros((8, 128), F32) for _ in range(2)]
            for j in range(20):
                here = block == j
                for a in range(2):
                    got[a] = jnp.where(here, lane_pick(wide(speed[pl.ds(a * 24 + j, 1), :]), lane), got[a])
            for a in range(2):
                weight = tab[pl.ds((G0 + 6 * a) * 16 + t * 8, 8), :]
                spread[half] = spread[half] + weight * (got[a] - flow_next[half][a])
        elevation_next = tuple(
            elevation[half] - spread[half] + FORCE_GAIN * flux[pl.ds(112 + half * 8, 8), :]
            for half in range(2)
        )
        return elevation_next, tuple(flow_next), ghost_next

    def mix(n, first_row, source, column0, accumulate):
        cells = pl.ds(pl.multiple_of(n * N_COLS, N_COLS), N_COLS)
        row = lax.broadcasted_iota(I32, (K_ROWS, N_COLS), 0) + first_row
        matrix = jnp.zeros((K_ROWS, N_COLS), F32)
        for m in range(EDGES):
            here = row == neighbours[pl.ds(m, 1), cells]
            matrix = matrix + jnp.where(here, lateral[pl.ds(m, 1), cells], 0.0)
        high = matrix.astype(BF16)
        low = (matrix - high.astype(F32)).astype(BF16)
        values = source[:, pl.ds(column0, K_ROWS)]
        both = jnp.dot(values, high, preferred_element_type=F32)
        added = both[:ROWS] + both[ROWS:] + jnp.dot(values[:ROWS], low, preferred_element_type=F32)
        if accumulate:
            added = total[:, cells] + added
        total[:, cells] = added

    def mix_own(n):
        mix(n, 0, parts, 0, False)

        def step(k, carry):
            first = pl.multiple_of(k * K_ROWS, K_ROWS)
            mix(n, first, parts, first, True)
            return carry

        lax.fori_loop(1, 4, step, 0)

    def mix_halo(n):
        mix(n, 2048, halo_parts, 0, True)
        sub = lax.broadcasted_iota(I32, (8, 128), 0)
        for part in range(2):
            c = n * 2 + part
            cells = pl.ds(pl.multiple_of(c * 128, 128), 128)
            weight = lateral[pl.ds(0, 1), cells]
            for m in range(1, EDGES):
                weight = weight + lateral[pl.ds(m, 1), cells]
            weight = wide(weight)
            layers = wide(count[pl.ds(c, 1), :])
            for g in range(ROWS // 8):
                rows = pl.ds(g * 8, 8)
                value = tracer[rows, cells]
                live = sub + (g * 8) % LAYERS < layers
                value = value + jnp.where(live, total[rows, cells] - weight * value, 0.0)
                profile[pl.ds(g * 128 + c, 8, stride=16), :] = value

    def layer(index):
        return pl.ds(pl.multiple_of(index * 16, 16), 16)

    def active(index):
        return (index < count[...]).astype(F32)

    def couple(index, upper):
        lower = thick_cells[layer(index + 1), :]
        return diffus_cells[layer(index), :] * 2.0 / (upper + lower) * active(index + 1)

    def vertical_gains():
        load_thick.wait()
        load_diffus.wait()
        for c in range(BLOCKS):
            cells = pl.ds(c * 128, 128)
            for g in range(8):
                thick_cells[pl.ds(g * 128 + c, 8, stride=16), :] = thick[pl.ds(g * 8, 8), cells]
                size = 8 if g < 7 else 7
                diffus_cells[pl.ds(g * 128 + c, size, stride=16), :] = diffus[pl.ds(g * 8, size), cells]

        def step(i, carry):
            below, gain = carry
            index = LAYERS - 1 - i
            here = thick_cells[layer(index), :]
            above = couple(index - 1, thick_cells[layer(index - 1), :])
            inverse = 1.0 / (here + above + below - below * gain)
            gain_here[layer(index), :] = here * inverse
            gain_below[layer(index), :] = below * inverse
            gain = above * inverse
            gain_above[layer(index), :] = gain
            return above, gain

        zero = jnp.zeros((16, 128), F32)
        return lax.fori_loop(0, LAYERS - 2, step, (zero, zero))

    def sweep_up():
        def step(i, carry):
            index = LAYERS - 1 - i
            here, below = gain_here[layer(index), :], gain_below[layer(index), :]
            out = []
            for t in range(TRACERS):
                rows = layer(t * LAYERS + index)
                value = here * profile[rows, :] + below * carry[t]
                profile[rows, :] = value
                out.append(value)
            return tuple(out)

        zero = jnp.zeros((16, 128), F32)
        return lax.fori_loop(0, LAYERS - 2, step, (zero,) * TRACERS)

    couple_one, gain_two = vertical_gains()

    def zero_state():
        elevation = tuple(surface[pl.ds(half * 8, 8), :] for half in range(2))
        flow = tuple(
            tuple(tab[pl.ds((VEL + a) * 16 + half * 8, 8), :] for a in range(2)) for half in range(2)
        )
        return elevation, flow

    def wait_round(s):
        pltpu.make_async_copy(inbox.at[s], inbox.at[s], round_recv.at[s]).wait()

    def one_round(s, state, work):
        elevation, flow, ghost_flow = state
        centres = [height[pl.ds(half * 8, 8), :] for half in range(2)]
        partial = own_sum(range(16), centres)
        work()
        wait_round(s)
        return take_round(s, elevation, flow, ghost_flow, partial)

    elevation, flow = zero_state()
    send_round(0, elevation)
    pltpu.make_async_copy(ghost_fixed, ghost_fixed, fixed_recv).wait()
    by_edge(ghost_fixed, ghost_lane, ghost_block, ghost_g)
    for b in range(4):
        for copy in range(2):
            for row, field in ((56, COR), (64, FORCE), (72, FORCE + 1), (80, VEL), (88, VEL + 1)):
                ghost_rows[pl.ds(row + copy * 4 + b, 1), :] = ghost_fixed[pl.ds(b * FIXED + field, 1), :]
    ghost_flow = (ghost_rows[pl.ds(80, 8), :], ghost_rows[pl.ds(88, 8), :])

    def early(s, state):
        state = one_round(s, state, lambda: mix_own(s))
        send_round(s + 1, state[0])
        return state

    state = lax.fori_loop(0, 4, early, (elevation, flow, ghost_flow))

    pltpu.make_async_copy(halo_in, halo_in, halo_recv).wait()
    for b in range(4):
        value = halo_in[b]
        high = value.astype(BF16)
        halo_parts[pl.ds(0, ROWS), pl.ds(b * 128, 128)] = high
        halo_parts[pl.ds(ROWS, ROWS), pl.ds(b * 128, 128)] = (value - high.astype(F32)).astype(BF16)

    def late_work(s):
        mix_own(s)
        mix_halo((s - 4) * 2)
        mix_halo((s - 4) * 2 + 1)

    def late(s, state):
        state = one_round(s, state, lambda: late_work(s))
        send_round(s + 1, state[0])
        return state

    state = lax.fori_loop(4, 7, late, state)
    tops = []

    def last_work():
        late_work(7)
        tops.append(sweep_up())

    elevation, flow, ghost_flow = one_round(7, state, last_work)
    values_two = tops[0]

    for half in range(2):
        final_surface[pl.ds(half * 8, 8), :] = elevation[half]
    for c in range(BLOCKS):
        final_velocity[0:1, pl.ds(c * 128, 128)] = speed[pl.ds(c, 1), :]
        final_velocity[1:2, pl.ds(c * 128, 128)] = speed[pl.ds(24 + c, 1), :]

    top = thick_cells[layer(0), :] + jnp.tanh(final_surface[...])
    second = thick_cells[layer(1), :]
    couple_zero = couple(0, top)
    inverse_one = 1.0 / (second + couple_zero + couple_one - couple_one * gain_two)
    gain_one = couple_zero * inverse_one
    inverse_zero = 1.0 / (top + couple_zero - couple_zero * gain_one)
    solved = []
    for t in range(TRACERS):
        rows_zero, rows_one = layer(t * LAYERS), layer(t * LAYERS + 1)
        value_one = (second * profile[rows_one, :] + couple_one * values_two[t]) * inverse_one
        right = top * profile[rows_zero, :] + FLUX_GAIN * flux[pl.ds(t * 16, 16), :]
        value_zero = (right + couple_zero * value_one) * inverse_zero
        profile[rows_zero, :] = value_zero
        value_one = value_one + gain_one * value_zero
        profile[rows_one, :] = value_one
        solved.append(value_one)

    def sweep_down(index, carry):
        above = gain_above[layer(index), :]
        out = []
        for t in range(TRACERS):
            rows = layer(t * LAYERS + index)
            value = profile[rows, :] + above * carry[t]
            profile[rows, :] = value
            out.append(value)
        return tuple(out)

    lax.fori_loop(2, LAYERS, sweep_down, tuple(solved))

    def place_out(c, carry):
        cells = pl.ds(pl.multiple_of(c * 128, 128), 128)
        for g in range(ROWS // 8):
            mixed[pl.ds(g * 8, 8), cells] = profile[pl.ds(g * 128 + c, 8, stride=16), :]
        return carry

    lax.fori_loop(0, BLOCKS, place_out, 0)

    pltpu.make_async_copy(inbox, inbox, round_send).wait()
    pltpu.make_async_copy(list_fixed, list_fixed, fixed_send).wait()
    pltpu.make_async_copy(halo_out, halo_out, halo_send_sem).wait()


def ocean(ocn_size, col_size, *operands):
    vmem = pl.BlockSpec(memory_space=pltpu.VMEM)
    hbm = pl.BlockSpec(memory_space=pl.ANY)

    def kernel(*refs):
        ocean_kernel(ocn_size, col_size, *refs)

    scratch = [
        pltpu.VMEM((LAYERS, 2048), F32),
        pltpu.VMEM((LAYERS - 1, 2048), F32),
        pltpu.VMEM((ROWS, 2048), F32),
        pltpu.VMEM((FIXED * 16, 128), F32),
        pltpu.VMEM((16, 8, 128), F32),
        pltpu.VMEM((128, 128), F32),
        pltpu.VMEM((4 * FIXED, 128), F32),
        pltpu.VMEM((4 * FIXED, 128), F32),
        pltpu.VMEM((96, 128), I32),
        pltpu.VMEM((96, 128), I32),
        pltpu.VMEM((24, 128), I32),
        pltpu.VMEM((24, 128), I32),
        pltpu.VMEM((48, 128), F32),
        pltpu.VMEM((24, 128), I32),
        pltpu.VMEM((24, 128), I32),
        pltpu.VMEM((48, 128), F32),
        pltpu.VMEM((24, 128), F32),
        pltpu.VMEM((48, 128), F32),
        pltpu.VMEM((96, 128), F32),
        pltpu.VMEM((SUBCYCLES, 4, 8, 128), F32),
        pltpu.VMEM((SUBCYCLES, 8, 8, 128), F32),
        pltpu.VMEM((4, ROWS, 128), F32),
        pltpu.VMEM((4, ROWS, 128), F32),
        pltpu.VMEM((2 * ROWS, 2048), BF16),
        pltpu.VMEM((2 * ROWS, 512), BF16),
        pltpu.VMEM((ROWS, 2048), F32),
        pltpu.VMEM((ROWS * 16, 128), F32),
        pltpu.VMEM((LAYERS * 16, 128), F32),
        pltpu.VMEM((LAYERS * 16, 128), F32),
        pltpu.VMEM((LAYERS * 16, 128), F32),
        pltpu.VMEM((LAYERS * 16, 128), F32),
        pltpu.VMEM((LAYERS * 16, 128), F32),
        pltpu.SemaphoreType.DMA((3,)),
        pltpu.SemaphoreType.DMA,
        pltpu.SemaphoreType.DMA,
        pltpu.SemaphoreType.DMA,
        pltpu.SemaphoreType.DMA,
        pltpu.SemaphoreType.DMA,
        pltpu.SemaphoreType.DMA((SUBCYCLES,)),
    ]
    return pl.pallas_call(
        kernel,
        name="ocean",
        out_shape=(
            jax.ShapeDtypeStruct((ROWS, 2048), F32),
            jax.ShapeDtypeStruct((16, 128), F32),
            jax.ShapeDtypeStruct((2, 2048), F32),
        ),
        in_specs=[vmem] * 11 + [hbm] * 3,
        out_specs=(vmem, vmem, vmem),
        scratch_shapes=scratch,
        compiler_params=pltpu.CompilerParams(
            collective_id=0, has_side_effects=True, vmem_limit_bytes=48 << 20
        ),
    )(*operands)


def solution(mesh):
    ocn_size, col_size = mesh.shape["ocn"], mesh.shape["col"]

    def per_device(
        air_flux,
        send_index,
        remap_column,
        remap_weight,
        halo_send,
        neighbours,
        gradient_weight,
        coriolis,
        sea_surface,
        velocity,
        lateral_weight,
        layer_count,
        thickness,
        diffusivity,
        tracers,
    ):
        outgoing = pl.pallas_call(
            pack_kernel,
            name="pack",
            out_shape=jax.ShapeDtypeStruct((128, 128), F32),
        )(air_flux, send_index.reshape(16, 128))
        arrived = lax.all_to_all(outgoing, ("ocn", "col"), split_axis=0, concat_axis=0, tiled=True)
        mixed, elevation, flow = ocean(
            ocn_size,
            col_size,
            arrived,
            remap_column,
            remap_weight,
            halo_send.reshape(4, 128),
            neighbours,
            gradient_weight,
            coriolis.reshape(16, 128),
            sea_surface.reshape(16, 128),
            velocity,
            lateral_weight,
            layer_count.reshape(16, 128),
            thickness,
            diffusivity,
            tracers.reshape(ROWS, 2048),
        )
        return mixed.reshape(TRACERS, LAYERS, 2048), elevation.reshape(2048), flow

    both = ("ocn", "col")
    placed = (
        P(None, both),
        P(both, None, None),
        P(None, both),
        P(None, both),
        P(both, None, None),
        P(None, both),
        P(None, None, both),
        P(both),
        P(both),
        P(None, both),
        P(None, both),
        P(both),
        P(None, both),
        P(None, both),
        P(None, None, both),
    )
    return jax.shard_map(
        per_device,
        mesh=mesh,
        in_specs=placed,
        out_specs=(P(None, None, both), P(both), P(None, both)),
        check_vma=False,
    )
```

```python
import jax
import jax.numpy as jnp
from jax import lax
from jax.experimental import pallas as pl
from jax.experimental.pallas import tpu as pltpu
from jax.sharding import PartitionSpec as P

F32 = jnp.float32
BF16 = jnp.bfloat16
I32 = jnp.int32
MESH = pl.DeviceIdType.MESH

SUBCYCLES = 8
LAYERS = 64
TRACERS = 4
ROWS = TRACERS * LAYERS
EDGES = 6
BLOCKS = 16
OFFSETS = (1, -1, 2, -2)
DISTANCES = (1, -1, 2, -2, 3, -3, 4, -4)
SEND_ORDER = (2, 3, 4, 5, 0, 1, 6, 7)
FLUX_GAIN = 2.0
FORCE_GAIN = 0.05

NB, G0, G1, COR, FORCE, VEL, FIXED = 0, 6, 12, 18, 19, 21, 24
N_COLS = 256
K_ROWS = 512


def wide(row):
    return jnp.broadcast_to(row, (8, 128))


def lane_pick(source, lane):
    return jnp.take_along_axis(source, lane, axis=1, mode="promise_in_bounds")


def ocean_kernel(
    ocn_size,
    col_size,
    air_hbm,
    send_hbm,
    column_hbm,
    remap_hbm,
    halo_send_hbm,
    neighbours_hbm,
    gradient_hbm,
    coriolis_hbm,
    surface_hbm,
    velocity_hbm,
    lateral_hbm,
    count_hbm,
    thick_hbm,
    diffusivity_hbm,
    tracer_hbm,
    rest_hbm,
    share_hbm,
    heads,
    final_surface,
    final_velocity,
    air,
    send_index,
    column,
    remap_weight,
    halo_lists,
    neighbours,
    gradient,
    coriolis,
    surface,
    velocity,
    lateral,
    count,
    thick,
    diffus,
    tracer,
    tab,
    square,
    outgoing,
    passing,
    arrived,
    received,
    flux,
    list_fixed,
    ghost_fixed,
    own_lane,
    own_block,
    list_lane,
    list_block,
    list_g,
    ghost_lane,
    ghost_block,
    ghost_g,
    height,
    speed,
    ghost_rows,
    message,
    inbox,
    halo_out,
    halo_in,
    parts,
    halo_parts,
    total,
    profile,
    thick_cells,
    diffus_cells,
    gain_here,
    gain_below,
    gain_above,
    load_sem,
    store_sem,
    col_send,
    col_recv,
    col_own,
    ocn_send,
    ocn_recv,
    ocn_own,
    fixed_send,
    fixed_recv,
    halo_send_sem,
    halo_recv,
    round_send,
    round_recv,
):
    devices = ocn_size * col_size
    ocn, col = lax.axis_index("ocn"), lax.axis_index("col")
    me = ocn * col_size + col

    def device(distance):
        target = lax.rem(me + (distance + devices), devices)
        return (target // col_size, lax.rem(target, col_size))

    def along_col(step):
        return lax.rem(col + step, col_size)

    def along_ocn(step):
        return lax.rem(ocn + step, ocn_size)

    sources = (
        air_hbm, send_hbm, halo_send_hbm, neighbours_hbm, gradient_hbm, coriolis_hbm, surface_hbm, velocity_hbm,
        tracer_hbm, column_hbm, remap_hbm, lateral_hbm, count_hbm, thick_hbm, diffusivity_hbm,
    )
    targets = (
        air, send_index, halo_lists, neighbours, gradient, coriolis, surface, velocity,
        tracer, column, remap_weight, lateral, count, thick, diffus,
    )
    loads = [
        pltpu.make_async_copy(source, target, load_sem.at[i])
        for i, (source, target) in enumerate(zip(sources, targets))
    ]
    for load in loads:
        load.start()

    barrier = pltpu.get_barrier_semaphore()
    for distance in DISTANCES:
        pl.semaphore_signal(barrier, inc=1, device_id=device(distance), device_id_type=MESH)
    for step in range(1, col_size):
        pl.semaphore_signal(barrier, inc=1, device_id=(ocn, along_col(step)), device_id_type=MESH)

    def greet(step, carry):
        pl.semaphore_signal(barrier, inc=1, device_id=(along_ocn(step), col), device_id_type=MESH)
        return carry

    lax.fori_loop(1, ocn_size, greet, 0)

    loads[0].wait()
    loads[1].wait()
    for slot in range(BLOCKS):
        index = wide(send_index[pl.ds(slot, 1), :])
        lane, block = index & 127, index >> 7
        got = jnp.zeros((8, 128), F32)
        for j in range(BLOCKS):
            got = jnp.where(block == j, lane_pick(air[:, pl.ds(j * 128, 128)], lane), got)
        square[pl.ds(slot, 8, stride=16), :] = got
    turned = square[...].T
    for target in range(ocn_size * col_size):
        outgoing[target // col_size, target % col_size, :, :] = turned[target : target + 1]
    pl.semaphore_wait(barrier, len(DISTANCES) + col_size - 1 + ocn_size - 1)
    for step in range(1, col_size):
        to = along_col(step)
        pltpu.make_async_remote_copy(
            outgoing.at[:, to], passing.at[col], col_send, col_recv, device_id=(ocn, to), device_id_type=MESH
        ).start()
    stay = pltpu.make_async_copy(outgoing.at[:, col], passing.at[col], col_own)
    stay.start()

    for load in loads[2:8]:
        load.wait()
    halo_send = halo_lists.at[0]

    for c in range(BLOCKS):
        cells = pl.ds(c * 128, 128)
        tab[pl.ds(NB * 16 + c, EDGES, stride=16), :] = neighbours[:, cells].astype(F32)
        for m in range(EDGES):
            tab[pl.ds((G0 + m) * 16 + c, 2, stride=16 * EDGES), :] = gradient[m, :, cells]
        tab[pl.ds(VEL * 16 + c, 2, stride=16), :] = velocity[:, cells]
    tab[pl.ds(COR * 16, 16), :] = coriolis[...]
    tab[pl.ds(23 * 16, 16), :] = jnp.zeros((16, 128), F32)
    for t in range(12):
        index = tab[pl.ds(t * 8, 8), :].astype(I32)
        own_lane[pl.ds(t * 8, 8), :] = index & 127
        own_block[pl.ds(t * 8, 8), :] = index >> 7

    pltpu.make_async_copy(passing.at[pl.ds(0, col_size - 1)], passing.at[pl.ds(0, col_size - 1)], col_recv).wait()
    stay.wait()

    def forward(step, carry):
        to = along_ocn(step)
        pltpu.make_async_remote_copy(
            passing.at[:, to], arrived.at[pl.ds(ocn * col_size, col_size)], ocn_send, ocn_recv,
            device_id=(to, col), device_id_type=MESH,
        ).start()
        return carry

    lax.fori_loop(1, ocn_size, forward, 0)
    stay = pltpu.make_async_copy(passing.at[:, ocn], arrived.at[pl.ds(ocn * col_size, col_size)], ocn_own)
    stay.start()

    def mix(n, first_row, source, column0, accumulate):
        cells = pl.ds(pl.multiple_of(n * N_COLS, N_COLS), N_COLS)
        row = lax.broadcasted_iota(I32, (K_ROWS, N_COLS), 0) + first_row
        matrix = jnp.zeros((K_ROWS, N_COLS), F32)
        for m in range(EDGES):
            here = row == neighbours[pl.ds(m, 1), cells]
            matrix = matrix + jnp.where(here, lateral[pl.ds(m, 1), cells], 0.0)
        high = matrix.astype(BF16)
        low = (matrix - high.astype(F32)).astype(BF16)
        values = source[:, pl.ds(column0, K_ROWS)]
        both = jnp.dot(values, high, preferred_element_type=F32)
        added = both[:ROWS] + both[ROWS:] + jnp.dot(values[:ROWS], low, preferred_element_type=F32)
        if accumulate:
            added = total[:, cells] + added
        total[:, cells] = added

    def mix_own(n):
        mix(n, 0, parts, 0, False)

        def step(k, carry):
            first = pl.multiple_of(k * K_ROWS, K_ROWS)
            mix(n, first, parts, first, True)
            return carry

        lax.fori_loop(1, 4, step, 0)

    def mix_halo(n):
        mix(n, 2048, halo_parts, 0, True)
        sub = lax.broadcasted_iota(I32, (8, 128), 0)
        for part in range(2):
            c = n * 2 + part
            cells = pl.ds(pl.multiple_of(c * 128, 128), 128)
            weight = lateral[pl.ds(0, 1), cells]
            for m in range(1, EDGES):
                weight = weight + lateral[pl.ds(m, 1), cells]
            weight = wide(weight)
            layers = wide(count[pl.ds(c, 1), :])
            for g in range(ROWS // 8):
                rows = pl.ds(g * 8, 8)
                value = tracer[rows, cells]
                live = sub + (g * 8) % LAYERS < layers
                value = value + jnp.where(live, total[rows, cells] - weight * value, 0.0)
                profile[pl.ds(g * 128 + c, 8, stride=16), :] = value

    loads[8].wait()
    for t in range(TRACERS):
        rows = pl.ds(t * LAYERS, LAYERS)
        value = tracer[rows, :]
        high = value.astype(BF16)
        parts[rows, :] = high
        parts[pl.ds(ROWS + t * LAYERS, LAYERS), :] = (value - high.astype(F32)).astype(BF16)
    place = lax.broadcasted_iota(I32, (2048, 128), 0)
    for b in range(4):
        chosen = jnp.where(place == halo_send[pl.ds(b, 1), :], 1.0, 0.0).astype(BF16)
        both = jnp.dot(parts[...], chosen, preferred_element_type=F32)
        halo_out[b] = both[:ROWS] + both[ROWS:]
    for b in range(4):
        pltpu.make_async_remote_copy(
            halo_out.at[b], halo_in.at[b], halo_send_sem, halo_recv,
            device_id=device(-OFFSETS[b]), device_id_type=MESH,
        ).start()

    def layer(index):
        return pl.ds(pl.multiple_of(index * 16, 16), 16)

    def active(index):
        return (index < count[...]).astype(F32)

    def couple(index, upper):
        lower = thick_cells[layer(index + 1), :]
        return diffus_cells[layer(index), :] * 2.0 / (upper + lower) * active(index + 1)

    def vertical_gains():
        for load in loads[12:15]:
            load.wait()
        for c in range(BLOCKS):
            cells = pl.ds(c * 128, 128)
            for g in range(8):
                thick_cells[pl.ds(g * 128 + c, 8, stride=16), :] = thick[pl.ds(g * 8, 8), cells]
                size = 8 if g < 7 else 7
                diffus_cells[pl.ds(g * 128 + c, size, stride=16), :] = diffus[pl.ds(g * 8, size), cells]

        def step(i, carry):
            below, gain = carry
            index = LAYERS - 1 - i
            here = thick_cells[layer(index), :]
            above = couple(index - 1, thick_cells[layer(index - 1), :])
            inverse = 1.0 / (here + above + below - below * gain)
            gain_here[layer(index), :] = here * inverse
            gain_below[layer(index), :] = below * inverse
            gain = above * inverse
            gain_above[layer(index), :] = gain
            return above, gain

        zero = jnp.zeros((16, 128), F32)
        return lax.fori_loop(0, LAYERS - 2, step, (zero, zero))

    lists = jnp.concatenate([halo_send[...]] * 2, axis=0)
    lists_lane, lists_block = lists & 127, lists >> 7

    def list_values(load):
        got = jnp.zeros((8, 128), F32)
        for j in range(BLOCKS):
            got = jnp.where(lists_block == j, lane_pick(wide(load(j)), lists_lane), got)
        return got

    def collect(field, carry):
        got = list_values(lambda j: tab[pl.ds(field * 16 + j, 1), :])
        list_fixed[pl.ds(field, 4, stride=FIXED), :] = got[:4]
        return carry

    lax.fori_loop(0, FORCE, collect, 0, unroll=4)
    lax.fori_loop(VEL, FIXED, collect, 0, unroll=3)
    couple_one, gain_two = vertical_gains()
    loads[11].wait()
    mix_own(BLOCKS // 2 - 1)

    for load in loads[9:11]:
        load.wait()
    others = pl.ds(0, devices - col_size)
    pltpu.make_async_copy(arrived.at[others], arrived.at[others], ocn_recv).wait()
    stay.wait()
    square[...] = arrived[:, 0, :].T
    for slot in range(BLOCKS):
        received[slot] = square[pl.ds(slot, 8, stride=16), :]

    def remap(c, carry):
        cells = pl.ds(pl.multiple_of(c * 128, 128), 128)
        result = jnp.zeros((8, 128), F32)
        for k in range(4):
            index = wide(column[pl.ds(k, 1), cells])
            lane, block = index >> 4, index & 15
            got = jnp.zeros((8, 128), F32)
            for j in range(BLOCKS):
                got = jnp.where(block == j, lane_pick(received[j], lane), got)
            result = result + wide(remap_weight[pl.ds(k, 1), cells]) * got
        flux[pl.ds(c, 8, stride=16), :] = result
        return carry

    lax.fori_loop(0, BLOCKS, remap, 0, unroll=4)
    tab[pl.ds(FORCE * 16, 32), :] = flux[pl.ds(64, 32), :]

    lax.fori_loop(FORCE, VEL, collect, 0, unroll=2)
    for b in range(4):
        rows = pl.ds(b * FIXED, FIXED)
        pltpu.make_async_remote_copy(
            list_fixed.at[rows], ghost_fixed.at[rows], fixed_send, fixed_recv,
            device_id=device(-OFFSETS[b]), device_id_type=MESH,
        ).start()

    def by_edge(fixed, lane_ref, block_ref, g_ref):
        for b in range(4):
            index = fixed[pl.ds(b * FIXED + NB, EDGES), :].astype(I32)
            lane_ref[pl.ds(b, EDGES, stride=4), :] = index & 127
            block_ref[pl.ds(b, EDGES, stride=4), :] = index >> 7
            g_ref[pl.ds(b, EDGES, stride=4), :] = fixed[pl.ds(b * FIXED + G0, EDGES), :]
            g_ref[pl.ds(24 + b, EDGES, stride=4), :] = fixed[pl.ds(b * FIXED + G1, EDGES), :]

    by_edge(list_fixed, list_lane, list_block, list_g)

    def both_halves(tile):
        return tile + pltpu.roll(tile, 4, 0)

    def send_round(s, elevation):
        for half in range(2):
            height[pl.ds(half * 8, 8), :] = elevation[half] + flux[pl.ds(96 + half * 8, 8), :]
        centre = list_values(lambda j: height[pl.ds(j, 1), :])
        first = jnp.zeros((8, 128), F32)
        second = jnp.zeros((8, 128), F32)
        for t in range(3):
            lane, block = list_lane[pl.ds(t * 8, 8), :], list_block[pl.ds(t * 8, 8), :]
            got = centre
            for j in range(BLOCKS):
                got = jnp.where(block == j, lane_pick(wide(height[pl.ds(j, 1), :]), lane), got)
            first = first + list_g[pl.ds(t * 8, 8), :] * (got - centre)
            second = second + list_g[pl.ds(24 + t * 8, 8), :] * (got - centre)
        first, second = both_halves(first), both_halves(second)
        for b in range(4):
            message[s, b, 0:4, :] = centre[:4]
            message[s, b, 4:5, :] = first[b : b + 1]
            message[s, b, 5:6, :] = second[b : b + 1]
            message[s, b, 6:8, :] = jnp.zeros((2, 128), F32)
        for k in SEND_ORDER:
            pltpu.make_async_remote_copy(
                message.at[s, k if k < 4 else 0], inbox.at[s, k], round_send, round_recv.at[s],
                device_id=device(-DISTANCES[k]), device_id_type=MESH,
            ).start()

    def own_sum(ranges, centres):
        sums = [[jnp.zeros((8, 128), F32) for _ in range(2)] for _ in range(2)]
        for t in range(12):
            half, rows = t % 2, pl.ds(t * 8, 8)
            lane, block = own_lane[rows, :], own_block[rows, :]
            got = centres[half]
            for j in ranges:
                got = jnp.where(block == j, lane_pick(wide(height[pl.ds(j, 1), :]), lane), got)
            apart = got - centres[half]
            for axis in range(2):
                weight = tab[pl.ds((G0 + 6 * axis) * 16 + t * 8, 8), :]
                sums[axis][half] = sums[axis][half] + weight * apart
        return sums

    def take_round(s, elevation, flow, ghost_flow, partial):
        for b in range(4):
            height[pl.ds(16 + b, 1), :] = inbox[s, b, b : b + 1, :]
            for copy in range(2):
                for source in range(4):
                    distance = OFFSETS[b] + OFFSETS[source]
                    if distance == 0:
                        row = message[s, 0, source : source + 1, :]
                    else:
                        row = inbox[s, DISTANCES.index(distance), source : source + 1, :]
                    ghost_rows[pl.ds(source * 8 + copy * 4 + b, 1), :] = row
                ghost_rows[pl.ds(32 + copy * 4 + b, 1), :] = inbox[s, b, b : b + 1, :]
                ghost_rows[pl.ds(40 + copy * 4 + b, 1), :] = inbox[s, b, 4:5, :]
                ghost_rows[pl.ds(48 + copy * 4 + b, 1), :] = inbox[s, b, 5:6, :]
        centres = [height[pl.ds(half * 8, 8), :] for half in range(2)]
        rest = own_sum(range(16, 20), centres)
        centre = ghost_rows[pl.ds(32, 8), :]
        ghost_sums = [jnp.zeros((8, 128), F32) for _ in range(2)]
        for t in range(3):
            rows = pl.ds(t * 8, 8)
            lane, block = ghost_lane[rows, :], ghost_block[rows, :]
            got = centre
            for j in range(4):
                got = jnp.where(block == 16 + j, lane_pick(ghost_rows[pl.ds(j * 8, 8), :], lane), got)
            for axis in range(2):
                ghost_sums[axis] = ghost_sums[axis] + ghost_g[pl.ds(axis * 24 + t * 8, 8), :] * (got - centre)
        ghost_sums = [both_halves(ghost_sums[a]) + ghost_rows[pl.ds(40 + 8 * a, 8), :] for a in range(2)]

        turn = ghost_rows[pl.ds(56, 8), :]
        ghost_next = (
            ghost_flow[0] - ghost_sums[0] + turn * ghost_flow[1] + FORCE_GAIN * ghost_rows[pl.ds(64, 8), :],
            ghost_flow[1] - ghost_sums[1] - turn * ghost_flow[0] + FORCE_GAIN * ghost_rows[pl.ds(72, 8), :],
        )
        flow_next = []
        for half in range(2):
            turn = tab[pl.ds(COR * 16 + half * 8, 8), :]
            force = [tab[pl.ds((FORCE + a) * 16 + half * 8, 8), :] for a in range(2)]
            grad = [partial[a][half] + rest[a][half] for a in range(2)]
            flow_next.append(
                (
                    flow[half][0] - grad[0] + turn * flow[half][1] + FORCE_GAIN * force[0],
                    flow[half][1] - grad[1] - turn * flow[half][0] + FORCE_GAIN * force[1],
                )
            )
        for a in range(2):
            for half in range(2):
                speed[pl.ds(a * 24 + half * 8, 8), :] = flow_next[half][a]
            speed[pl.ds(a * 24 + 16, 8), :] = ghost_next[a]
        spread = [jnp.zeros((8, 128), F32) for _ in range(2)]
        for t in range(12):
            half, rows = t % 2, pl.ds(t * 8, 8)
            lane, block = own_lane[rows, :], own_block[rows, :]
            got = [jnp.zeros((8, 128), F32) for _ in range(2)]
            for j in range(20):
                here = block == j
                for a in range(2):
                    got[a] = jnp.where(here, lane_pick(wide(speed[pl.ds(a * 24 + j, 1), :]), lane), got[a])
            for a in range(2):
                weight = tab[pl.ds((G0 + 6 * a) * 16 + t * 8, 8), :]
                spread[half] = spread[half] + weight * (got[a] - flow_next[half][a])
        elevation_next = tuple(
            elevation[half] - spread[half] + FORCE_GAIN * flux[pl.ds(112 + half * 8, 8), :]
            for half in range(2)
        )
        return elevation_next, tuple(flow_next), ghost_next

    def sweep_up():
        def step(i, carry):
            index = LAYERS - 1 - i
            here, below = gain_here[layer(index), :], gain_below[layer(index), :]
            out = []
            for t in range(TRACERS):
                rows = layer(t * LAYERS + index)
                value = here * profile[rows, :] + below * carry[t]
                profile[rows, :] = value
                out.append(value)
            return tuple(out)

        zero = jnp.zeros((16, 128), F32)
        return lax.fori_loop(0, LAYERS - 2, step, (zero,) * TRACERS)

    def zero_state():
        elevation = tuple(surface[pl.ds(half * 8, 8), :] for half in range(2))
        flow = tuple(
            tuple(tab[pl.ds((VEL + a) * 16 + half * 8, 8), :] for a in range(2)) for half in range(2)
        )
        return elevation, flow

    def wait_round(s):
        pltpu.make_async_copy(inbox.at[s], inbox.at[s], round_recv.at[s]).wait()

    def one_round(s, state, work):
        elevation, flow, ghost_flow = state
        centres = [height[pl.ds(half * 8, 8), :] for half in range(2)]
        partial = own_sum(range(16), centres)
        work()
        wait_round(s)
        return take_round(s, elevation, flow, ghost_flow, partial)

    elevation, flow = zero_state()
    send_round(0, elevation)
    pltpu.make_async_copy(ghost_fixed, ghost_fixed, fixed_recv).wait()
    by_edge(ghost_fixed, ghost_lane, ghost_block, ghost_g)
    for b in range(4):
        for copy in range(2):
            for row, field in ((56, COR), (64, FORCE), (72, FORCE + 1), (80, VEL), (88, VEL + 1)):
                ghost_rows[pl.ds(row + copy * 4 + b, 1), :] = ghost_fixed[pl.ds(b * FIXED + field, 1), :]
    ghost_flow = (ghost_rows[pl.ds(80, 8), :], ghost_rows[pl.ds(88, 8), :])

    def early(s, state):
        state = one_round(s, state, lambda: mix_own(s))
        send_round(s + 1, state[0])
        return state

    state = lax.fori_loop(0, 2, early, (elevation, flow, ghost_flow))

    pltpu.make_async_copy(halo_in, halo_in, halo_recv).wait()
    for b in range(4):
        value = halo_in[b]
        high = value.astype(BF16)
        halo_parts[pl.ds(0, ROWS), pl.ds(b * 128, 128)] = high
        halo_parts[pl.ds(ROWS, ROWS), pl.ds(b * 128, 128)] = (value - high.astype(F32)).astype(BF16)

    def late_work(s):
        mix_own(s)

        def step(n, carry):
            mix_halo(n)
            return carry

        lax.fori_loop((s - 2) * 8 // 5, (s - 1) * 8 // 5, step, 0)

    def late(s, state):
        state = one_round(s, state, lambda: late_work(s))
        send_round(s + 1, state[0])
        return state

    state = lax.fori_loop(2, 7, late, state)

    def sweep_down(index, carry):
        above = gain_above[layer(index), :]
        share = above * carry[0]
        gain_above[layer(index), :] = share
        out = []
        for t in range(TRACERS):
            rows = layer(t * LAYERS + index)
            value = profile[rows, :] + above * carry[1 + t]
            profile[rows, :] = value
            out.append(value)
        return (share, *out)

    def place_out(c, carry):
        cells = pl.ds(pl.multiple_of(c * 128, 128), 128)
        deep = lax.broadcasted_iota(I32, (8, 128), 0) > 1
        for g in range(ROWS // 8):
            value = profile[pl.ds(g * 128 + c, 8, stride=16), :]
            if g % 8 == 0:
                value = jnp.where(deep, value, 0.0)
            total[pl.ds(g * 8, 8), cells] = value
        for g in range(LAYERS // 8):
            thick[pl.ds(g * 8, 8), cells] = gain_above[pl.ds(g * 128 + c, 8, stride=16), :]
        return carry

    stores = (
        pltpu.make_async_copy(total, rest_hbm, store_sem.at[0]),
        pltpu.make_async_copy(thick, share_hbm, store_sem.at[1]),
    )
    tops = []

    def last_work():
        tops.append(sweep_up())
        zero, one = jnp.zeros((16, 128), F32), jnp.ones((16, 128), F32)
        gain_above[layer(0), :] = zero
        gain_above[layer(1), :] = one
        lax.fori_loop(2, LAYERS, sweep_down, (one,) + (zero,) * TRACERS)
        lax.fori_loop(0, BLOCKS, place_out, 0)
        for store in stores:
            store.start()

    elevation, flow, ghost_flow = one_round(7, state, last_work)
    values_two = tops[0]

    for half in range(2):
        final_surface[pl.ds(half * 8, 8), :] = elevation[half]
    for c in range(BLOCKS):
        final_velocity[0:1, pl.ds(c * 128, 128)] = speed[pl.ds(c, 1), :]
        final_velocity[1:2, pl.ds(c * 128, 128)] = speed[pl.ds(24 + c, 1), :]

    top = thick_cells[layer(0), :] + jnp.tanh(final_surface[...])
    second = thick_cells[layer(1), :]
    couple_zero = couple(0, top)
    inverse_one = 1.0 / (second + couple_zero + couple_one - couple_one * gain_two)
    gain_one = couple_zero * inverse_one
    inverse_zero = 1.0 / (top + couple_zero - couple_zero * gain_one)
    for t in range(TRACERS):
        rows_zero, rows_one = layer(t * LAYERS), layer(t * LAYERS + 1)
        value_one = (second * profile[rows_one, :] + couple_one * values_two[t]) * inverse_one
        right = top * profile[rows_zero, :] + FLUX_GAIN * flux[pl.ds(t * 16, 16), :]
        value_zero = (right + couple_zero * value_one) * inverse_zero
        square[pl.ds(t * 16, 16), :] = value_zero
        square[pl.ds(64 + t * 16, 16), :] = value_one + gain_one * value_zero
    for c in range(BLOCKS):
        heads[:, pl.ds(c * 128, 128)] = square[pl.ds(c, 8, stride=16), :]

    for store in stores:
        store.wait()
    pltpu.make_async_copy(inbox, inbox, round_send).wait()
    pltpu.make_async_copy(list_fixed, list_fixed, fixed_send).wait()
    pltpu.make_async_copy(halo_out, halo_out, halo_send_sem).wait()
    pltpu.make_async_copy(passing.at[pl.ds(0, col_size - 1)], passing.at[pl.ds(0, col_size - 1)], col_send).wait()
    pltpu.make_async_copy(arrived.at[others], arrived.at[others], ocn_send).wait()


def finish_kernel(
    rest_hbm, share_hbm, heads_hbm, surface_hbm, flow_hbm, mixed_hbm, surface_out, flow_out,
    rest, share, heads, load_sem, store_sem,
):
    loads = [
        pltpu.make_async_copy(share_hbm, share, load_sem.at[0]),
        pltpu.make_async_copy(heads_hbm, heads, load_sem.at[1]),
    ]
    stores = [
        pltpu.make_async_copy(surface_hbm, surface_out, store_sem.at[0]),
        pltpu.make_async_copy(flow_hbm, flow_out, store_sem.at[1]),
    ]
    for t in range(TRACERS):
        rows = pl.ds(t * LAYERS, LAYERS)
        loads.append(pltpu.make_async_copy(rest_hbm.at[rows], rest.at[rows], load_sem.at[2 + t]))
        stores.append(pltpu.make_async_copy(rest.at[rows], mixed_hbm.at[rows], store_sem.at[2 + t]))
    for copy in loads + stores[:2]:
        copy.start()
    loads[0].wait()
    loads[1].wait()
    sub = lax.broadcasted_iota(I32, (8, 2048), 0)
    for t in range(TRACERS):
        loads[2 + t].wait()
        head = jnp.broadcast_to(heads[pl.ds(4 + t, 1), :], (8, 2048))
        for g in range(LAYERS // 8):
            rows = pl.ds(t * LAYERS + g * 8, 8)
            value = rest[rows, :] + share[pl.ds(g * 8, 8), :] * head
            if g == 0:
                value = jnp.where(sub == 0, jnp.broadcast_to(heads[pl.ds(t, 1), :], (8, 2048)), value)
            rest[rows, :] = value
        stores[2 + t].start()
    for store in stores:
        store.wait()


def finish(*operands):
    hbm = pl.BlockSpec(memory_space=pl.ANY)
    return pl.pallas_call(
        finish_kernel,
        name="finish",
        out_shape=(
            jax.ShapeDtypeStruct((ROWS, 2048), F32),
            jax.ShapeDtypeStruct((16, 128), F32),
            jax.ShapeDtypeStruct((2, 2048), F32),
        ),
        in_specs=[hbm] * 5,
        out_specs=(hbm,) * 3,
        scratch_shapes=[
            pltpu.VMEM((ROWS, 2048), F32),
            pltpu.VMEM((LAYERS, 2048), F32),
            pltpu.VMEM((8, 2048), F32),
            pltpu.SemaphoreType.DMA((6,)),
            pltpu.SemaphoreType.DMA((6,)),
        ],
        compiler_params=pltpu.CompilerParams(vmem_limit_bytes=60 << 20),
    )(*operands)


def ocean(ocn_size, col_size, *operands):
    vmem = pl.BlockSpec(memory_space=pltpu.VMEM)
    hbm = pl.BlockSpec(memory_space=pl.ANY)

    def kernel(*refs):
        ocean_kernel(ocn_size, col_size, *refs)

    scratch = [
        pltpu.VMEM((8, 2048), F32),
        pltpu.VMEM((16, 128), I32),
        pltpu.VMEM((4, 2048), I32),
        pltpu.VMEM((4, 2048), F32),
        pltpu.VMEM((1, 4, 128), I32),
        pltpu.VMEM((EDGES, 2048), I32),
        pltpu.VMEM((EDGES, 2, 2048), F32),
        pltpu.VMEM((16, 128), F32),
        pltpu.VMEM((16, 128), F32),
        pltpu.VMEM((2, 2048), F32),
        pltpu.VMEM((EDGES, 2048), F32),
        pltpu.VMEM((16, 128), I32),
        pltpu.VMEM((LAYERS, 2048), F32),
        pltpu.VMEM((LAYERS - 1, 2048), F32),
        pltpu.VMEM((ROWS, 2048), F32),
        pltpu.VMEM((FIXED * 16, 128), F32),
        pltpu.VMEM((128, 128), F32),
        pltpu.VMEM((ocn_size, col_size, 1, 128), F32),
        pltpu.VMEM((col_size, ocn_size, 1, 128), F32),
        pltpu.VMEM((ocn_size * col_size, 1, 128), F32),
        pltpu.VMEM((16, 8, 128), F32),
        pltpu.VMEM((128, 128), F32),
        pltpu.VMEM((4 * FIXED, 128), F32),
        pltpu.VMEM((4 * FIXED, 128), F32),
        pltpu.VMEM((96, 128), I32),
        pltpu.VMEM((96, 128), I32),
        pltpu.VMEM((24, 128), I32),
        pltpu.VMEM((24, 128), I32),
        pltpu.VMEM((48, 128), F32),
        pltpu.VMEM((24, 128), I32),
        pltpu.VMEM((24, 128), I32),
        pltpu.VMEM((48, 128), F32),
        pltpu.VMEM((24, 128), F32),
        pltpu.VMEM((48, 128), F32),
        pltpu.VMEM((96, 128), F32),
        pltpu.VMEM((SUBCYCLES, 4, 8, 128), F32),
        pltpu.VMEM((SUBCYCLES, 8, 8, 128), F32),
        pltpu.VMEM((4, ROWS, 128), F32),
        pltpu.VMEM((4, ROWS, 128), F32),
        pltpu.VMEM((2 * ROWS, 2048), BF16),
        pltpu.VMEM((2 * ROWS, 512), BF16),
        pltpu.VMEM((ROWS, 2048), F32),
        pltpu.VMEM((ROWS * 16, 128), F32),
        pltpu.VMEM((LAYERS * 16, 128), F32),
        pltpu.VMEM((LAYERS * 16, 128), F32),
        pltpu.VMEM((LAYERS * 16, 128), F32),
        pltpu.VMEM((LAYERS * 16, 128), F32),
        pltpu.VMEM((LAYERS * 16, 128), F32),
        pltpu.SemaphoreType.DMA((15,)),
        pltpu.SemaphoreType.DMA((2,)),
        pltpu.SemaphoreType.DMA,
        pltpu.SemaphoreType.DMA,
        pltpu.SemaphoreType.DMA,
        pltpu.SemaphoreType.DMA,
        pltpu.SemaphoreType.DMA,
        pltpu.SemaphoreType.DMA,
        pltpu.SemaphoreType.DMA,
        pltpu.SemaphoreType.DMA,
        pltpu.SemaphoreType.DMA,
        pltpu.SemaphoreType.DMA,
        pltpu.SemaphoreType.DMA,
        pltpu.SemaphoreType.DMA((SUBCYCLES,)),
    ]
    return pl.pallas_call(
        kernel,
        name="ocean",
        out_shape=(
            jax.ShapeDtypeStruct((ROWS, 2048), F32),
            jax.ShapeDtypeStruct((LAYERS, 2048), F32),
            jax.ShapeDtypeStruct((8, 2048), F32),
            jax.ShapeDtypeStruct((16, 128), F32),
            jax.ShapeDtypeStruct((2, 2048), F32),
        ),
        in_specs=[hbm] * 15,
        out_specs=(hbm, hbm, vmem, vmem, vmem),
        scratch_shapes=scratch,
        compiler_params=pltpu.CompilerParams(
            collective_id=0, has_side_effects=True, vmem_limit_bytes=60 << 20
        ),
    )(*operands)


def solution(mesh):
    ocn_size, col_size = mesh.shape["ocn"], mesh.shape["col"]

    def per_device(
        air_flux,
        send_index,
        remap_column,
        remap_weight,
        halo_send,
        neighbours,
        gradient_weight,
        coriolis,
        sea_surface,
        velocity,
        lateral_weight,
        layer_count,
        thickness,
        diffusivity,
        tracers,
    ):
        solved = ocean(
            ocn_size,
            col_size,
            air_flux,
            send_index[0].T,
            remap_column,
            remap_weight,
            halo_send,
            neighbours,
            jnp.swapaxes(gradient_weight, 0, 1),
            coriolis.reshape(16, 128),
            sea_surface.reshape(16, 128),
            velocity,
            lateral_weight,
            layer_count.reshape(16, 128),
            thickness,
            diffusivity,
            tracers.reshape(ROWS, 2048),
        )
        mixed, elevation, flow = finish(*solved)
        return mixed.reshape(TRACERS, LAYERS, 2048), elevation.reshape(2048), flow

    both = ("ocn", "col")
    placed = (
        P(None, both),
        P(both, None, None),
        P(None, both),
        P(None, both),
        P(both, None, None),
        P(None, both),
        P(None, None, both),
        P(both),
        P(both),
        P(None, both),
        P(None, both),
        P(both),
        P(None, both),
        P(None, both),
        P(None, None, both),
    )
    return jax.shard_map(
        per_device,
        mesh=mesh,
        in_specs=placed,
        out_specs=(P(None, None, both), P(both), P(None, both)),
        check_vma=False,
    )
```

```python
import jax
import jax.numpy as jnp
from jax import lax
from jax.experimental import pallas as pl
from jax.experimental.pallas import tpu as pltpu
from jax.sharding import PartitionSpec as P

F32 = jnp.float32
BF16 = jnp.bfloat16
I32 = jnp.int32
MESH = pl.DeviceIdType.MESH

SUBCYCLES = 8
LAYERS = 64
TRACERS = 4
ROWS = TRACERS * LAYERS
EDGES = 6
BLOCKS = 16
OFFSETS = (1, -1, 2, -2)
DISTANCES = (1, -1, 2, -2, 3, -3, 4, -4)
SEND_ORDER = (2, 3, 4, 5, 0, 1, 6, 7)
FLUX_GAIN = 2.0
FORCE_GAIN = 0.05

NB, G0, G1, COR, VEL, FORCE, FIXED = 0, 6, 12, 18, 19, 21, 24
N_COLS = 256
K_ROWS = 1024


def wide(row):
    return jnp.broadcast_to(row, (8, 128))


def lane_pick(source, lane):
    return jnp.take_along_axis(source, lane, axis=1, mode="promise_in_bounds")


def ocean_kernel(
    ocn_size,
    col_size,
    air_hbm,
    send_hbm,
    column_hbm,
    remap_hbm,
    halo_send_hbm,
    neighbours_hbm,
    gradient_hbm,
    coriolis_hbm,
    surface_hbm,
    velocity_hbm,
    lateral_hbm,
    count_hbm,
    thick_hbm,
    diffusivity_hbm,
    tracer_hbm,
    rest_hbm,
    share_hbm,
    heads,
    final_surface,
    final_velocity,
    air,
    send_index,
    column,
    remap_weight,
    halo_lists,
    neighbours,
    gradient,
    coriolis,
    surface,
    velocity,
    lateral,
    count,
    thick,
    diffus,
    tracer,
    tab,
    square,
    outgoing,
    passing,
    arrived,
    received,
    halves,
    flux,
    list_fixed,
    ghost_fixed,
    force_out,
    force_in,
    own_lane,
    own_block,
    list_lane,
    list_block,
    list_g,
    ghost_lane,
    ghost_block,
    ghost_g,
    height,
    speed,
    ghost_rows,
    message,
    near_box,
    far_box,
    halo_out,
    halo_in,
    parts,
    halo_parts,
    total,
    profile,
    thick_cells,
    diffus_cells,
    gain_here,
    gain_below,
    gain_above,
    tops,
    load_sem,
    store_sem,
    col_send,
    col_recv,
    col_own,
    ocn_send,
    ocn_recv,
    ocn_own,
    fixed_send,
    fixed_recv,
    force_send,
    force_recv,
    halo_send_sem,
    halo_recv,
    near_send,
    near_recv,
    far_send,
    far_recv,
):
    devices = ocn_size * col_size
    ocn, col = lax.axis_index("ocn"), lax.axis_index("col")
    me = ocn * col_size + col

    def device(distance):
        target = lax.rem(me + (distance + devices), devices)
        return (target // col_size, lax.rem(target, col_size))

    def along_col(step):
        return lax.rem(col + step, col_size)

    def along_ocn(step):
        return lax.rem(ocn + step, ocn_size)

    sources = (
        air_hbm, send_hbm, halo_send_hbm, neighbours_hbm, gradient_hbm, coriolis_hbm, surface_hbm, velocity_hbm,
        tracer_hbm, column_hbm, remap_hbm, lateral_hbm, count_hbm, thick_hbm, diffusivity_hbm,
    )
    targets = (
        air, send_index, halo_lists, neighbours, gradient, coriolis, surface, velocity,
        tracer, column, remap_weight, lateral, count, thick, diffus,
    )
    loads = [
        pltpu.make_async_copy(source, target, load_sem.at[i])
        for i, (source, target) in enumerate(zip(sources, targets))
    ]
    for load in loads[:2]:
        load.start()

    barrier = pltpu.get_barrier_semaphore()
    for distance in DISTANCES:
        pl.semaphore_signal(barrier, inc=1, device_id=device(distance), device_id_type=MESH)
    for step in range(1, col_size):
        pl.semaphore_signal(barrier, inc=1, device_id=(ocn, along_col(step)), device_id_type=MESH)

    def greet(step, carry):
        pl.semaphore_signal(barrier, inc=1, device_id=(along_ocn(step), col), device_id_type=MESH)
        return carry

    lax.fori_loop(1, ocn_size, greet, 0)
    for load in loads[2:]:
        load.start()

    loads[0].wait()
    loads[1].wait()
    for slot in range(BLOCKS):
        index = wide(send_index[pl.ds(slot, 1), :])
        lane, block = index & 127, index >> 7
        got = jnp.zeros((8, 128), F32)
        for j in range(BLOCKS):
            got = jnp.where(block == j, lane_pick(air[:, pl.ds(j * 128, 128)], lane), got)
        square[pl.ds(slot, 8, stride=16), :] = got
    turned = square[...].T
    for target in range(ocn_size * col_size):
        outgoing[target // col_size, target % col_size, :, :] = turned[target : target + 1]
    pl.semaphore_wait(barrier, len(DISTANCES) + col_size - 1 + ocn_size - 1)
    for step in range(1, col_size):
        to = along_col(step)
        pltpu.make_async_remote_copy(
            outgoing.at[:, to], passing.at[col], col_send, col_recv, device_id=(ocn, to), device_id_type=MESH
        ).start()
    stay = pltpu.make_async_copy(outgoing.at[:, col], passing.at[col], col_own)
    stay.start()

    for load in loads[2:8]:
        load.wait()
    halo_send = halo_lists.at[0]

    for c in range(BLOCKS):
        cells = pl.ds(c * 128, 128)
        tab[pl.ds(NB * 16 + c, EDGES, stride=16), :] = neighbours[:, cells].astype(F32)
        for m in range(EDGES):
            tab[pl.ds((G0 + m) * 16 + c, 2, stride=16 * EDGES), :] = gradient[m, :, cells]
        tab[pl.ds(VEL * 16 + c, 2, stride=16), :] = velocity[:, cells]
    tab[pl.ds(COR * 16, 16), :] = coriolis[...]
    tab[pl.ds(FORCE * 16, 48), :] = jnp.zeros((48, 128), F32)
    for t in range(12):
        index = tab[pl.ds(t * 8, 8), :].astype(I32)
        own_lane[pl.ds(t * 8, 8), :] = index & 127
        own_block[pl.ds(t * 8, 8), :] = index >> 7

    pltpu.make_async_copy(passing.at[pl.ds(0, col_size - 1)], passing.at[pl.ds(0, col_size - 1)], col_recv).wait()
    stay.wait()

    def forward(i, carry):
        step = 1 + (i + 11) % (ocn_size - 1)
        to = along_ocn(step)
        pltpu.make_async_remote_copy(
            passing.at[:, to], arrived.at[pl.ds(ocn * col_size, col_size)], ocn_send, ocn_recv,
            device_id=(to, col), device_id_type=MESH,
        ).start()
        return carry

    lax.fori_loop(0, ocn_size - 1, forward, 0)
    stay = pltpu.make_async_copy(passing.at[:, ocn], arrived.at[pl.ds(ocn * col_size, col_size)], ocn_own)
    stay.start()

    lists = jnp.concatenate([halo_send[...]] * 2, axis=0)
    lists_lane, lists_block = lists & 127, lists >> 7

    def list_values(load):
        got = jnp.zeros((8, 128), F32)
        for j in range(BLOCKS):
            got = jnp.where(lists_block == j, lane_pick(wide(load(j)), lists_lane), got)
        return got

    def collect(field, carry):
        got = list_values(lambda j: tab[pl.ds(field * 16 + j, 1), :])
        list_fixed[pl.ds(field, 4, stride=FIXED), :] = got[:4]
        return carry

    lax.fori_loop(0, FIXED, collect, 0, unroll=4)
    for b in range(4):
        rows = pl.ds(b * FIXED, FIXED)
        pltpu.make_async_remote_copy(
            list_fixed.at[rows], ghost_fixed.at[rows], fixed_send, fixed_recv,
            device_id=device(-OFFSETS[b]), device_id_type=MESH,
        ).start()

    def by_edge(fixed, lane_ref, block_ref, g_ref):
        for b in range(4):
            index = fixed[pl.ds(b * FIXED + NB, EDGES), :].astype(I32)
            lane_ref[pl.ds(b, EDGES, stride=4), :] = index & 127
            block_ref[pl.ds(b, EDGES, stride=4), :] = index >> 7
            g_ref[pl.ds(b, EDGES, stride=4), :] = fixed[pl.ds(b * FIXED + G0, EDGES), :]
            g_ref[pl.ds(24 + b, EDGES, stride=4), :] = fixed[pl.ds(b * FIXED + G1, EDGES), :]

    by_edge(list_fixed, list_lane, list_block, list_g)

    def merge_lateral():
        index = [neighbours[pl.ds(m, 1), :] for m in range(EDGES)]
        weight = [lateral[pl.ds(m, 1), :] for m in range(EDGES)]
        for m in range(1, EDGES):
            moved = index[m] == index[0]
            weight[0] = weight[0] + jnp.where(moved, weight[m], 0.0)
            for k in range(1, m):
                same = jnp.logical_and(index[m] == index[k], jnp.logical_not(moved))
                weight[k] = weight[k] + jnp.where(same, weight[m], 0.0)
                moved = jnp.logical_or(moved, same)
            weight[m] = jnp.where(moved, 0.0, weight[m])
        for m in range(EDGES):
            lateral[pl.ds(m, 1), :] = weight[m]

    def mix(n, first_row, source, column0, count_rows):
        cells = pl.ds(pl.multiple_of(n * N_COLS, N_COLS), N_COLS)
        row = lax.broadcasted_iota(I32, (count_rows, N_COLS), 0) + first_row
        matrix = jnp.zeros((count_rows, N_COLS), F32)
        for m in reversed(range(EDGES)):
            here = row == neighbours[pl.ds(m, 1), cells]
            matrix = jnp.where(here, lateral[pl.ds(m, 1), cells], matrix)
        high = matrix.astype(BF16)
        low = (matrix - high.astype(F32)).astype(BF16)
        values = source[:, pl.ds(column0, count_rows)]
        both = jnp.dot(values, high, preferred_element_type=F32)
        added = both[:ROWS] + both[ROWS:] + jnp.dot(values[:ROWS], low, preferred_element_type=F32)
        total[:, cells] = total[:, cells] + added

    def mix_own(n):
        total[:, pl.ds(pl.multiple_of(n * N_COLS, N_COLS), N_COLS)] = jnp.zeros((ROWS, N_COLS), F32)

        def step(k, carry):
            first = pl.multiple_of(k * K_ROWS, K_ROWS)
            mix(n, first, parts, first, K_ROWS)
            return carry

        lax.fori_loop(0, 2048 // K_ROWS, step, 0)

    def mix_halo(n):
        mix(n, 2048, halo_parts, 0, 512)
        sub = lax.broadcasted_iota(I32, (8, 128), 0)
        for part in range(2):
            c = n * 2 + part
            cells = pl.ds(pl.multiple_of(c * 128, 128), 128)
            weight = lateral[pl.ds(0, 1), cells]
            for m in range(1, EDGES):
                weight = weight + lateral[pl.ds(m, 1), cells]
            weight = wide(weight)
            layers = wide(count[pl.ds(c, 1), :])
            for g in range(ROWS // 8):
                rows = pl.ds(g * 8, 8)
                value = tracer[rows, cells]
                live = sub + (g * 8) % LAYERS < layers
                value = value + jnp.where(live, total[rows, cells] - weight * value, 0.0)
                profile[pl.ds(g * 128 + c, 8, stride=16), :] = value

    loads[8].wait()
    for t in range(TRACERS):
        rows = pl.ds(t * LAYERS, LAYERS)
        value = tracer[rows, :]
        high = value.astype(BF16)
        parts[rows, :] = high
        parts[pl.ds(ROWS + t * LAYERS, LAYERS), :] = (value - high.astype(F32)).astype(BF16)
    place = lax.broadcasted_iota(I32, (2048, 256), 0)
    for pair in range(2):
        lists = [halo_send[pl.ds(pair * 2 + b, 1), :] for b in range(2)]
        chosen = jnp.where(place == jnp.concatenate(lists, axis=1), 1.0, 0.0).astype(BF16)
        both = jnp.dot(parts[...], chosen, preferred_element_type=F32)
        both = both[:ROWS] + both[ROWS:]
        for b in range(2):
            halo_out[pair * 2 + b] = both[:, b * 128 : b * 128 + 128]

    def send_halo(t):
        rows = pl.ds(pl.multiple_of(t * LAYERS, LAYERS), LAYERS)
        for b in range(4):
            pltpu.make_async_remote_copy(
                halo_out.at[b, rows], halo_in.at[b, rows], halo_send_sem, halo_recv,
                device_id=device(-OFFSETS[b]), device_id_type=MESH,
            ).start()

    def layer(index):
        return pl.ds(pl.multiple_of(index * 16, 16), 16)

    def active(index):
        return (index < count[...]).astype(F32)

    def couple(index, upper):
        lower = thick_cells[layer(index + 1), :]
        return diffus_cells[layer(index), :] * 2.0 / (upper + lower) * active(index + 1)

    def vertical_gains():
        for load in loads[12:15]:
            load.wait()
        for c in range(BLOCKS):
            cells = pl.ds(c * 128, 128)
            for g in range(8):
                thick_cells[pl.ds(g * 128 + c, 8, stride=16), :] = thick[pl.ds(g * 8, 8), cells]
                size = 8 if g < 7 else 7
                diffus_cells[pl.ds(g * 128 + c, size, stride=16), :] = diffus[pl.ds(g * 8, size), cells]

        def step(i, carry):
            below, gain = carry
            index = LAYERS - 1 - i
            here = thick_cells[layer(index), :]
            above = couple(index - 1, thick_cells[layer(index - 1), :])
            inverse = 1.0 / (here + above + below - below * gain)
            gain_here[layer(index), :] = here * inverse
            gain_below[layer(index), :] = below * inverse
            gain = above * inverse
            gain_above[layer(index), :] = gain
            return above, gain

        zero = jnp.zeros((16, 128), F32)
        return lax.fori_loop(0, LAYERS - 2, step, (zero, zero))

    couple_one, gain_two = vertical_gains()
    loads[11].wait()
    merge_lateral()

    for load in loads[9:11]:
        load.wait()
    others = pl.ds(0, devices - col_size)
    pltpu.make_async_copy(arrived.at[others], arrived.at[others], ocn_recv).wait()
    stay.wait()
    square[...] = arrived[:, 0, :].T
    for slot in range(BLOCKS):
        received[slot] = square[pl.ds(slot, 8, stride=16), :]

    def remap(start):
        upper = lax.broadcasted_iota(I32, (8, 128), 0) < 4
        for slot in range(BLOCKS):
            tile = received[slot]
            other = pltpu.roll(tile, 4, 0)
            halves[slot] = jnp.where(upper, tile, other) if start == 0 else jnp.where(upper, other, tile)

        def step(pair, carry):
            cells = [pl.ds(pl.multiple_of(pair * 256 + half * 128, 128), 128) for half in range(2)]
            result = jnp.zeros((8, 128), F32)
            for k in range(4):
                index = jnp.where(upper, wide(column[pl.ds(k, 1), cells[0]]), wide(column[pl.ds(k, 1), cells[1]]))
                weight = jnp.where(
                    upper, wide(remap_weight[pl.ds(k, 1), cells[0]]), wide(remap_weight[pl.ds(k, 1), cells[1]])
                )
                lane, block = index >> 4, index & 15
                got = jnp.zeros((8, 128), F32)
                for j in range(BLOCKS):
                    got = jnp.where(block == j, lane_pick(halves[j], lane), got)
                result = result + weight * got
            flux[pl.ds(start * 16 + pair * 2, 4, stride=16), :] = result[:4]
            flux[pl.ds(start * 16 + pair * 2 + 1, 4, stride=16), :] = result[4:]
            return carry

        lax.fori_loop(0, BLOCKS // 2, step, 0, unroll=4)

    remap(4)
    tab[pl.ds(FORCE * 16, 32), :] = flux[pl.ds(64, 32), :]

    sub = lax.broadcasted_iota(I32, (8, 128), 0)
    forces = [list_values(lambda j, a=a: tab[pl.ds((FORCE + a) * 16 + j, 1), :]) for a in range(2)]
    force_out[...] = jnp.where(sub < 4, forces[0], forces[1])
    for b in range(4):
        pltpu.make_async_remote_copy(
            force_out, force_in.at[b], force_send, force_recv.at[b],
            device_id=device(-OFFSETS[b]), device_id_type=MESH,
        ).start()


    def both_halves(tile):
        return tile + pltpu.roll(tile, 4, 0)

    def send_round(s, elevation):
        for half in range(2):
            height[pl.ds(half * 8, 8), :] = elevation[half] + flux[pl.ds(96 + half * 8, 8), :]
        centre = list_values(lambda j: height[pl.ds(j, 1), :])
        first = jnp.zeros((8, 128), F32)
        second = jnp.zeros((8, 128), F32)
        for t in range(3):
            lane, block = list_lane[pl.ds(t * 8, 8), :], list_block[pl.ds(t * 8, 8), :]
            got = jnp.zeros((8, 128), F32)
            for j in range(BLOCKS):
                got = jnp.where(block == j, lane_pick(wide(height[pl.ds(j, 1), :]), lane), got)
            got = jnp.where(block < BLOCKS, got, centre)
            first = first + list_g[pl.ds(t * 8, 8), :] * (got - centre)
            second = second + list_g[pl.ds(24 + t * 8, 8), :] * (got - centre)
        first, second = both_halves(first), both_halves(second)
        sub = lax.broadcasted_iota(I32, (8, 128), 0)
        message[s, pl.ds(0, 8), :] = jnp.where(sub < 4, centre, first)
        message[s, pl.ds(8, 8), :] = second
        for k in SEND_ORDER:
            if k < 4:
                pltpu.make_async_remote_copy(
                    message.at[s], near_box.at[s, k], near_send, near_recv.at[s],
                    device_id=device(-DISTANCES[k]), device_id_type=MESH,
                ).start()
            else:
                pltpu.make_async_remote_copy(
                    message.at[s, pl.ds(0, 8)], far_box.at[s, k - 4], far_send, far_recv.at[s],
                    device_id=device(-DISTANCES[k]), device_id_type=MESH,
                ).start()

    def own_sum(rows_of, centres):
        sums = [[jnp.zeros((8, 128), F32) for _ in range(2)] for _ in range(2)]
        for t in range(12):
            half, rows = t % 2, pl.ds(t * 8, 8)
            lane, block = own_lane[rows, :], own_block[rows, :]
            got = centres[half]
            for j, load in rows_of:
                got = jnp.where(block == j, lane_pick(load(), lane), got)
            apart = got - centres[half]
            for axis in range(2):
                weight = tab[pl.ds((G0 + 6 * axis) * 16 + t * 8, 8), :]
                sums[axis][half] = sums[axis][half] + weight * apart
        return sums

    def take_round(s, elevation, flow, ghost_flow, partial):
        def near(b, row):
            return wide(near_box[s, b, pl.ds(row, 1), :])

        def listed(distance, row):
            if distance == 0:
                return wide(message[s, pl.ds(row, 1), :])
            k = DISTANCES.index(distance)
            return near(k, row) if k < 4 else wide(far_box[s, k - 4, pl.ds(row, 1), :])

        which = lax.broadcasted_iota(I32, (8, 128), 0) & 3

        def by_list(load):
            out = load(0)
            for b in range(1, 4):
                out = jnp.where(which == b, load(b), out)
            return out

        centres = [height[pl.ds(half * 8, 8), :] for half in range(2)]
        rest = own_sum([(16 + b, lambda b=b: near(b, b)) for b in range(4)], centres)
        centre = by_list(lambda b: near(b, b))
        second_hand = [by_list(lambda b: listed(OFFSETS[b] + OFFSETS[j], j)) for j in range(4)]
        ghost_sums = [jnp.zeros((8, 128), F32) for _ in range(2)]
        for t in range(3):
            rows = pl.ds(t * 8, 8)
            lane, block = ghost_lane[rows, :], ghost_block[rows, :]
            got = centre
            for j in range(4):
                got = jnp.where(block == 16 + j, lane_pick(second_hand[j], lane), got)
            for axis in range(2):
                ghost_sums[axis] = ghost_sums[axis] + ghost_g[pl.ds(axis * 24 + t * 8, 8), :] * (got - centre)
        ghost_sums = [
            both_halves(ghost_sums[a]) + by_list(lambda b: near(b, 4 + 4 * a + b)) for a in range(2)
        ]

        turn = ghost_rows[pl.ds(0, 8), :]
        ghost_next = (
            ghost_flow[0] - ghost_sums[0] + turn * ghost_flow[1] + FORCE_GAIN * ghost_rows[pl.ds(8, 8), :],
            ghost_flow[1] - ghost_sums[1] - turn * ghost_flow[0] + FORCE_GAIN * ghost_rows[pl.ds(16, 8), :],
        )
        flow_next = []
        for half in range(2):
            turn = tab[pl.ds(COR * 16 + half * 8, 8), :]
            force = [tab[pl.ds((FORCE + a) * 16 + half * 8, 8), :] for a in range(2)]
            grad = [partial[a][half] + rest[a][half] for a in range(2)]
            flow_next.append(
                (
                    flow[half][0] - grad[0] + turn * flow[half][1] + FORCE_GAIN * force[0],
                    flow[half][1] - grad[1] - turn * flow[half][0] + FORCE_GAIN * force[1],
                )
            )
        for a in range(2):
            for half in range(2):
                speed[pl.ds(a * 24 + half * 8, 8), :] = flow_next[half][a]
            speed[pl.ds(a * 24 + 16, 8), :] = ghost_next[a]
        spread = [jnp.zeros((8, 128), F32) for _ in range(2)]
        for t in range(12):
            half, rows = t % 2, pl.ds(t * 8, 8)
            lane, block = own_lane[rows, :], own_block[rows, :]
            got = [jnp.zeros((8, 128), F32) for _ in range(2)]
            for j in range(20):
                here = block == j
                for a in range(2):
                    got[a] = jnp.where(here, lane_pick(wide(speed[pl.ds(a * 24 + j, 1), :]), lane), got[a])
            for a in range(2):
                weight = tab[pl.ds((G0 + 6 * a) * 16 + t * 8, 8), :]
                spread[half] = spread[half] + weight * (got[a] - flow_next[half][a])
        elevation_next = tuple(
            elevation[half] - spread[half] + FORCE_GAIN * flux[pl.ds(112 + half * 8, 8), :]
            for half in range(2)
        )
        return elevation_next, tuple(flow_next), ghost_next

    def sweep_up():
        def step(i, carry):
            index = LAYERS - 1 - i
            here, below = gain_here[layer(index), :], gain_below[layer(index), :]
            out = []
            for t in range(TRACERS):
                rows = layer(t * LAYERS + index)
                value = here * profile[rows, :] + below * carry[t]
                profile[rows, :] = value
                out.append(value)
            return tuple(out)

        zero = jnp.zeros((16, 128), F32)
        return lax.fori_loop(0, LAYERS - 2, step, (zero,) * TRACERS)

    def zero_state():
        elevation = tuple(surface[pl.ds(half * 8, 8), :] for half in range(2))
        flow = tuple(
            tuple(tab[pl.ds((VEL + a) * 16 + half * 8, 8), :] for a in range(2)) for half in range(2)
        )
        return elevation, flow

    def one_round(s, state, work):
        elevation, flow, ghost_flow = state
        centres = [height[pl.ds(half * 8, 8), :] for half in range(2)]
        own_rows = [(j, lambda j=j: wide(height[pl.ds(j, 1), :])) for j in range(16)]
        partial = own_sum(own_rows, centres)
        work()
        pltpu.make_async_copy(far_box.at[s], far_box.at[s], far_recv.at[s]).wait()
        pltpu.make_async_copy(near_box.at[s], near_box.at[s], near_recv.at[s]).wait()

        @pl.when(s == 0)
        def _():
            for b in range(4):
                pltpu.make_async_copy(force_in.at[b], force_in.at[b], force_recv.at[b]).wait()
                for a in range(2):
                    for copy in range(2):
                        row = force_in[b, pl.ds(a * 4 + b, 1), :]
                        ghost_rows[pl.ds(8 + a * 8 + copy * 4 + b, 1), :] = row

        return take_round(s, elevation, flow, ghost_flow, partial)

    elevation, flow = zero_state()
    send_round(0, elevation)
    pltpu.make_async_copy(ghost_fixed, ghost_fixed, fixed_recv).wait()
    by_edge(ghost_fixed, ghost_lane, ghost_block, ghost_g)
    for b in range(4):
        for copy in range(2):
            for row, field in ((0, COR), (24, VEL), (32, VEL + 1)):
                ghost_rows[pl.ds(row + copy * 4 + b, 1), :] = ghost_fixed[pl.ds(b * FIXED + field, 1), :]
    ghost_flow = (ghost_rows[pl.ds(24, 8), :], ghost_rows[pl.ds(32, 8), :])

    def split_halo():
        pltpu.make_async_copy(halo_in, halo_in, halo_recv).wait()
        for b in range(4):
            value = halo_in[b]
            high = value.astype(BF16)
            halo_parts[pl.ds(0, ROWS), pl.ds(b * 128, 128)] = high
            halo_parts[pl.ds(ROWS, ROWS), pl.ds(b * 128, 128)] = (value - high.astype(F32)).astype(BF16)

    def sweep_down(index, carry):
        above = gain_above[layer(index), :]
        share = above * carry[0]
        gain_above[layer(index), :] = share
        out = []
        for t in range(TRACERS):
            rows = layer(t * LAYERS + index)
            value = profile[rows, :] + above * carry[1 + t]
            profile[rows, :] = value
            out.append(value)
        return (share, *out)

    def place_out(c, carry):
        cells = pl.ds(pl.multiple_of(c * 128, 128), 128)
        deep = lax.broadcasted_iota(I32, (8, 128), 0) > 1
        for g in range(ROWS // 8):
            value = profile[pl.ds(g * 128 + c, 8, stride=16), :]
            if g % 8 == 0:
                value = jnp.where(deep, value, 0.0)
            total[pl.ds(g * 8, 8), cells] = value
        for g in range(LAYERS // 8):
            thick[pl.ds(g * 8, 8), cells] = gain_above[pl.ds(g * 128 + c, 8, stride=16), :]
        return carry

    stores = (
        pltpu.make_async_copy(total, rest_hbm, store_sem.at[0]),
        pltpu.make_async_copy(thick, share_hbm, store_sem.at[1]),
    )

    def solve_below():
        values = sweep_up()
        for t in range(TRACERS):
            tops[pl.ds(t * 16, 16), :] = values[t]
        zero, one = jnp.zeros((16, 128), F32), jnp.ones((16, 128), F32)
        gain_above[layer(0), :] = zero
        gain_above[layer(1), :] = one
        lax.fori_loop(2, LAYERS, sweep_down, (one,) + (zero,) * TRACERS)
        lax.fori_loop(0, BLOCKS, place_out, 0)
        for store in stores:
            store.start()

    def tracer_work(s):
        @pl.when(s < 4)
        def _():
            send_halo(s)

            def step(i, carry):
                mix_own(2 * s + i)
                return carry

            lax.fori_loop(0, 2, step, 0)

        @pl.when(s == 4)
        def _():
            split_halo()
            remap(0)

        @pl.when(jnp.logical_and(s >= 4, s < 6))
        def _():
            def step(i, carry):
                mix_halo(4 * (s - 4) + i)
                return carry

            lax.fori_loop(0, 4, step, 0)

        @pl.when(s == 6)
        def _():
            solve_below()

    def subcycle(s, state):
        state = one_round(s, state, lambda: tracer_work(s))

        @pl.when(s < SUBCYCLES - 1)
        def _():
            send_round(s + 1, state[0])

        return state

    elevation, flow, ghost_flow = lax.fori_loop(0, SUBCYCLES, subcycle, (elevation, flow, ghost_flow))

    for half in range(2):
        final_surface[pl.ds(half * 8, 8), :] = elevation[half]
    for c in range(BLOCKS):
        final_velocity[0:1, pl.ds(c * 128, 128)] = speed[pl.ds(c, 1), :]
        final_velocity[1:2, pl.ds(c * 128, 128)] = speed[pl.ds(24 + c, 1), :]

    top = thick_cells[layer(0), :] + jnp.tanh(final_surface[...])
    second = thick_cells[layer(1), :]
    couple_zero = couple(0, top)
    inverse_one = 1.0 / (second + couple_zero + couple_one - couple_one * gain_two)
    gain_one = couple_zero * inverse_one
    inverse_zero = 1.0 / (top + couple_zero - couple_zero * gain_one)
    for t in range(TRACERS):
        rows_zero, rows_one = layer(t * LAYERS), layer(t * LAYERS + 1)
        value_one = (second * profile[rows_one, :] + couple_one * tops[pl.ds(t * 16, 16), :]) * inverse_one
        right = top * profile[rows_zero, :] + FLUX_GAIN * flux[pl.ds(t * 16, 16), :]
        value_zero = (right + couple_zero * value_one) * inverse_zero
        square[pl.ds(t * 16, 16), :] = value_zero
        square[pl.ds(64 + t * 16, 16), :] = value_one + gain_one * value_zero
    for c in range(BLOCKS):
        heads[:, pl.ds(c * 128, 128)] = square[pl.ds(c, 8, stride=16), :]

    for store in stores:
        store.wait()
    pltpu.make_async_copy(near_box, near_box, near_send).wait()
    pltpu.make_async_copy(far_box, far_box, far_send).wait()
    pltpu.make_async_copy(list_fixed, list_fixed, fixed_send).wait()
    pltpu.make_async_copy(force_in, force_in, force_send).wait()
    pltpu.make_async_copy(halo_out, halo_out, halo_send_sem).wait()
    pltpu.make_async_copy(passing.at[pl.ds(0, col_size - 1)], passing.at[pl.ds(0, col_size - 1)], col_send).wait()
    pltpu.make_async_copy(arrived.at[others], arrived.at[others], ocn_send).wait()


def finish_kernel(
    rest_hbm, share_hbm, heads_hbm, surface_hbm, flow_hbm, mixed_hbm, surface_out, flow_out,
    rest, share, heads, load_sem, store_sem,
):
    loads = [
        pltpu.make_async_copy(share_hbm, share, load_sem.at[0]),
        pltpu.make_async_copy(heads_hbm, heads, load_sem.at[1]),
    ]
    stores = [
        pltpu.make_async_copy(surface_hbm, surface_out, store_sem.at[0]),
        pltpu.make_async_copy(flow_hbm, flow_out, store_sem.at[1]),
    ]
    for t in range(TRACERS):
        rows = pl.ds(t * LAYERS, LAYERS)
        loads.append(pltpu.make_async_copy(rest_hbm.at[rows], rest.at[rows], load_sem.at[2 + t]))
        stores.append(pltpu.make_async_copy(rest.at[rows], mixed_hbm.at[rows], store_sem.at[2 + t]))
    for copy in loads + stores[:2]:
        copy.start()
    loads[0].wait()
    loads[1].wait()
    sub = lax.broadcasted_iota(I32, (8, 2048), 0)
    for t in range(TRACERS):
        loads[2 + t].wait()
        head = jnp.broadcast_to(heads[pl.ds(4 + t, 1), :], (8, 2048))
        for g in range(LAYERS // 8):
            rows = pl.ds(t * LAYERS + g * 8, 8)
            value = rest[rows, :] + share[pl.ds(g * 8, 8), :] * head
            if g == 0:
                value = jnp.where(sub == 0, jnp.broadcast_to(heads[pl.ds(t, 1), :], (8, 2048)), value)
            rest[rows, :] = value
        stores[2 + t].start()
    for store in stores:
        store.wait()


def finish(*operands):
    hbm = pl.BlockSpec(memory_space=pl.ANY)
    return pl.pallas_call(
        finish_kernel,
        name="finish",
        out_shape=(
            jax.ShapeDtypeStruct((ROWS, 2048), F32),
            jax.ShapeDtypeStruct((16, 128), F32),
            jax.ShapeDtypeStruct((2, 2048), F32),
        ),
        in_specs=[hbm] * 5,
        out_specs=(hbm,) * 3,
        scratch_shapes=[
            pltpu.VMEM((ROWS, 2048), F32),
            pltpu.VMEM((LAYERS, 2048), F32),
            pltpu.VMEM((8, 2048), F32),
            pltpu.SemaphoreType.DMA((6,)),
            pltpu.SemaphoreType.DMA((6,)),
        ],
        compiler_params=pltpu.CompilerParams(vmem_limit_bytes=60 << 20),
    )(*operands)


def ocean(ocn_size, col_size, *operands):
    vmem = pl.BlockSpec(memory_space=pltpu.VMEM)
    hbm = pl.BlockSpec(memory_space=pl.ANY)

    def kernel(*refs):
        ocean_kernel(ocn_size, col_size, *refs)

    scratch = [
        pltpu.VMEM((8, 2048), F32),
        pltpu.VMEM((16, 128), I32),
        pltpu.VMEM((4, 2048), I32),
        pltpu.VMEM((4, 2048), F32),
        pltpu.VMEM((1, 4, 128), I32),
        pltpu.VMEM((EDGES, 2048), I32),
        pltpu.VMEM((EDGES, 2, 2048), F32),
        pltpu.VMEM((16, 128), F32),
        pltpu.VMEM((16, 128), F32),
        pltpu.VMEM((2, 2048), F32),
        pltpu.VMEM((EDGES, 2048), F32),
        pltpu.VMEM((16, 128), I32),
        pltpu.VMEM((LAYERS, 2048), F32),
        pltpu.VMEM((LAYERS - 1, 2048), F32),
        pltpu.VMEM((ROWS, 2048), F32),
        pltpu.VMEM((FIXED * 16, 128), F32),
        pltpu.VMEM((128, 128), F32),
        pltpu.VMEM((ocn_size, col_size, 1, 128), F32),
        pltpu.VMEM((col_size, ocn_size, 1, 128), F32),
        pltpu.VMEM((ocn_size * col_size, 1, 128), F32),
        pltpu.VMEM((16, 8, 128), F32),
        pltpu.VMEM((16, 8, 128), F32),
        pltpu.VMEM((128, 128), F32),
        pltpu.VMEM((4 * FIXED, 128), F32),
        pltpu.VMEM((4 * FIXED, 128), F32),
        pltpu.VMEM((8, 128), F32),
        pltpu.VMEM((4, 8, 128), F32),
        pltpu.VMEM((96, 128), I32),
        pltpu.VMEM((96, 128), I32),
        pltpu.VMEM((24, 128), I32),
        pltpu.VMEM((24, 128), I32),
        pltpu.VMEM((48, 128), F32),
        pltpu.VMEM((24, 128), I32),
        pltpu.VMEM((24, 128), I32),
        pltpu.VMEM((48, 128), F32),
        pltpu.VMEM((16, 128), F32),
        pltpu.VMEM((48, 128), F32),
        pltpu.VMEM((40, 128), F32),
        pltpu.VMEM((SUBCYCLES, 16, 128), F32),
        pltpu.VMEM((SUBCYCLES, 4, 16, 128), F32),
        pltpu.VMEM((SUBCYCLES, 4, 8, 128), F32),
        pltpu.VMEM((4, ROWS, 128), F32),
        pltpu.VMEM((4, ROWS, 128), F32),
        pltpu.VMEM((2 * ROWS, 2048), BF16),
        pltpu.VMEM((2 * ROWS, 512), BF16),
        pltpu.VMEM((ROWS, 2048), F32),
        pltpu.VMEM((ROWS * 16, 128), F32),
        pltpu.VMEM((LAYERS * 16, 128), F32),
        pltpu.VMEM((LAYERS * 16, 128), F32),
        pltpu.VMEM((LAYERS * 16, 128), F32),
        pltpu.VMEM((LAYERS * 16, 128), F32),
        pltpu.VMEM((LAYERS * 16, 128), F32),
        pltpu.VMEM((TRACERS * 16, 128), F32),
        pltpu.SemaphoreType.DMA((15,)),
        pltpu.SemaphoreType.DMA((2,)),
        pltpu.SemaphoreType.DMA,
        pltpu.SemaphoreType.DMA,
        pltpu.SemaphoreType.DMA,
        pltpu.SemaphoreType.DMA,
        pltpu.SemaphoreType.DMA,
        pltpu.SemaphoreType.DMA,
        pltpu.SemaphoreType.DMA,
        pltpu.SemaphoreType.DMA,
        pltpu.SemaphoreType.DMA,
        pltpu.SemaphoreType.DMA((4,)),
        pltpu.SemaphoreType.DMA,
        pltpu.SemaphoreType.DMA,
        pltpu.SemaphoreType.DMA,
        pltpu.SemaphoreType.DMA((SUBCYCLES,)),
        pltpu.SemaphoreType.DMA,
        pltpu.SemaphoreType.DMA((SUBCYCLES,)),
    ]
    return pl.pallas_call(
        kernel,
        name="ocean",
        out_shape=(
            jax.ShapeDtypeStruct((ROWS, 2048), F32),
            jax.ShapeDtypeStruct((LAYERS, 2048), F32),
            jax.ShapeDtypeStruct((8, 2048), F32),
            jax.ShapeDtypeStruct((16, 128), F32),
            jax.ShapeDtypeStruct((2, 2048), F32),
        ),
        in_specs=[hbm] * 15,
        out_specs=(hbm, hbm, vmem, vmem, vmem),
        scratch_shapes=scratch,
        compiler_params=pltpu.CompilerParams(
            collective_id=0, has_side_effects=True, vmem_limit_bytes=60 << 20
        ),
    )(*operands)


def solution(mesh):
    ocn_size, col_size = mesh.shape["ocn"], mesh.shape["col"]

    def per_device(
        air_flux,
        send_index,
        remap_column,
        remap_weight,
        halo_send,
        neighbours,
        gradient_weight,
        coriolis,
        sea_surface,
        velocity,
        lateral_weight,
        layer_count,
        thickness,
        diffusivity,
        tracers,
    ):
        solved = ocean(
            ocn_size,
            col_size,
            air_flux,
            send_index[0].T,
            remap_column,
            remap_weight,
            halo_send,
            neighbours,
            jnp.swapaxes(gradient_weight, 0, 1),
            coriolis.reshape(16, 128),
            sea_surface.reshape(16, 128),
            velocity,
            lateral_weight,
            layer_count.reshape(16, 128),
            thickness,
            diffusivity,
            tracers.reshape(ROWS, 2048),
        )
        mixed, elevation, flow = finish(*solved)
        return mixed.reshape(TRACERS, LAYERS, 2048), elevation.reshape(2048), flow

    both = ("ocn", "col")
    placed = (
        P(None, both),
        P(both, None, None),
        P(None, both),
        P(None, both),
        P(both, None, None),
        P(None, both),
        P(None, None, both),
        P(both),
        P(both),
        P(None, both),
        P(None, both),
        P(both),
        P(None, both),
        P(None, both),
        P(None, None, both),
    )
    return jax.shard_map(
        per_device,
        mesh=mesh,
        in_specs=placed,
        out_specs=(P(None, None, both), P(both), P(None, both)),
        check_vma=False,
    )
```

```python
import jax
import jax.numpy as jnp
from jax import lax
from jax.experimental import pallas as pl
from jax.experimental.pallas import tpu as pltpu
from jax.sharding import PartitionSpec as P

F32 = jnp.float32
BF16 = jnp.bfloat16
I32 = jnp.int32
MESH = pl.DeviceIdType.MESH

SUBCYCLES = 8
LAYERS = 64
TRACERS = 4
ROWS = TRACERS * LAYERS
EDGES = 6
BLOCKS = 16
OFFSETS = (1, -1, 2, -2)
DISTANCES = (1, -1, 2, -2, 3, -3, 4, -4)
FLUX_GAIN = 2.0
FORCE_GAIN = 0.05

NB, G0, G1, COR, VEL, FORCE, FIXED = 0, 6, 12, 18, 19, 21, 24
N_COLS = 256
K_ROWS = 1024
PIECE = 32


def wide(row):
    return jnp.broadcast_to(row, (8, 128))


def lane_pick(source, lane):
    return jnp.take_along_axis(source, lane, axis=1, mode="promise_in_bounds")


def ocean_kernel(
    ocn_size,
    col_size,
    air_hbm,
    send_hbm,
    column_hbm,
    remap_hbm,
    halo_send_hbm,
    neighbours_hbm,
    gradient_hbm,
    coriolis_hbm,
    surface_hbm,
    velocity_hbm,
    lateral_hbm,
    count_hbm,
    thick_hbm,
    diffusivity_hbm,
    tracer_hbm,
    rest_hbm,
    share_hbm,
    heads,
    final_surface,
    final_velocity,
    air,
    send_index,
    column,
    remap_weight,
    halo_lists,
    neighbours,
    gradient,
    coriolis,
    surface,
    velocity,
    lateral,
    count,
    thick,
    diffus,
    tracer,
    tab,
    square,
    outgoing,
    passing,
    arrived,
    received,
    halves,
    flux,
    list_fixed,
    ghost_fixed,
    force_out,
    force_in,
    own_lane,
    own_block,
    list_lane,
    list_block,
    list_g,
    ghost_lane,
    ghost_block,
    ghost_g,
    height,
    speed,
    ghost_rows,
    message,
    near_box,
    far_box,
    halo_out,
    halo_in,
    parts,
    halo_parts,
    total,
    profile,
    thick_cells,
    diffus_cells,
    gain_here,
    gain_below,
    gain_above,
    tops,
    load_sem,
    store_sem,
    col_send,
    col_recv,
    col_own,
    ocn_send,
    ocn_recv,
    ocn_own,
    fixed_send,
    fixed_recv,
    force_send,
    force_recv,
    halo_send_sem,
    halo_recv,
    near_send,
    near_recv,
    far_send,
    far_recv,
):
    devices = ocn_size * col_size
    ocn, col = lax.axis_index("ocn"), lax.axis_index("col")
    me = ocn * col_size + col
    odd = lax.rem(ocn, 2)

    def device(distance):
        target = lax.rem(me + (distance + devices), devices)
        return (target // col_size, lax.rem(target, col_size))

    column_size = 2 * col_size
    chips = ocn_size // 2
    chip, place_in_column = ocn // 2, odd * col_size + col

    def in_column(step):
        to = lax.rem(place_in_column + step, column_size)
        return to, (chip * 2 + to // col_size, lax.rem(to, col_size))

    def across(step):
        to = lax.rem(chip + step, chips)
        return to, (to * 2 + odd, col)

    sources = (
        air_hbm, send_hbm, halo_send_hbm, neighbours_hbm, gradient_hbm, coriolis_hbm, surface_hbm, velocity_hbm,
        tracer_hbm, column_hbm, remap_hbm, lateral_hbm, count_hbm, thick_hbm, diffusivity_hbm,
    )
    targets = (
        air, send_index, halo_lists, neighbours, gradient, coriolis, surface, velocity,
        tracer, column, remap_weight, lateral, count, thick, diffus,
    )
    loads = [
        pltpu.make_async_copy(source, target, load_sem.at[i])
        for i, (source, target) in enumerate(zip(sources, targets))
    ]
    for load in loads[:2]:
        load.start()

    barrier = pltpu.get_barrier_semaphore()
    for distance in DISTANCES:
        pl.semaphore_signal(barrier, inc=1, device_id=device(distance), device_id_type=MESH)
    for step in range(1, column_size):
        pl.semaphore_signal(barrier, inc=1, device_id=in_column(step)[1], device_id_type=MESH)
    for step in range(1, chips):
        pl.semaphore_signal(barrier, inc=1, device_id=across(step)[1], device_id_type=MESH)
    for load in loads[2:]:
        load.start()

    loads[0].wait()
    loads[1].wait()
    for slot in range(BLOCKS):
        index = wide(send_index[pl.ds(slot, 1), :])
        lane, block = index & 127, index >> 7
        got = jnp.zeros((8, 128), F32)
        for j in range(BLOCKS):
            got = jnp.where(block == j, lane_pick(air[:, pl.ds(j * 128, 128)], lane), got)
        square[pl.ds(slot, 8, stride=16), :] = got
    turned = square[...].T
    for target in range(ocn_size * col_size):
        outgoing[target // column_size, target % column_size, :, :] = turned[target : target + 1]
    pl.semaphore_wait(barrier, len(DISTANCES) + column_size - 1 + chips - 1)
    for i in range(column_size - 1):
        to, target = in_column(1 + (i + 1) % (column_size - 1))
        pltpu.make_async_remote_copy(
            outgoing.at[:, to], passing.at[place_in_column], col_send, col_recv,
            device_id=target, device_id_type=MESH,
        ).start()
    stay = pltpu.make_async_copy(outgoing.at[:, place_in_column], passing.at[place_in_column], col_own)
    stay.start()

    for load in loads[2:8]:
        load.wait()
    halo_send = halo_lists.at[0]

    for c in range(BLOCKS):
        cells = pl.ds(c * 128, 128)
        tab[pl.ds(NB * 16 + c, EDGES, stride=16), :] = neighbours[:, cells].astype(F32)
        for m in range(EDGES):
            tab[pl.ds((G0 + m) * 16 + c, 2, stride=16 * EDGES), :] = gradient[m, :, cells]
        tab[pl.ds(VEL * 16 + c, 2, stride=16), :] = velocity[:, cells]
    tab[pl.ds(COR * 16, 16), :] = coriolis[...]
    tab[pl.ds(FORCE * 16, 48), :] = jnp.zeros((48, 128), F32)
    for t in range(12):
        index = tab[pl.ds(t * 8, 8), :].astype(I32)
        own_lane[pl.ds(t * 8, 8), :] = index & 127
        own_block[pl.ds(t * 8, 8), :] = index >> 7

    gathered = passing.at[pl.ds(0, column_size - 1)]
    pltpu.make_async_copy(gathered, gathered, col_recv).wait()
    stay.wait()
    landing = arrived.at[pl.ds(chip * column_size, column_size)]
    for i in range(chips - 1):
        to, target = across(1 + (i + chips // 2 - 3) % (chips - 1))
        pltpu.make_async_remote_copy(
            passing.at[:, to], landing, ocn_send, ocn_recv, device_id=target, device_id_type=MESH
        ).start()
    stay = pltpu.make_async_copy(passing.at[:, chip], landing, ocn_own)
    stay.start()

    lists = jnp.concatenate([halo_send[...]] * 2, axis=0)
    lists_lane, lists_block = lists & 127, lists >> 7

    def list_values(load):
        got = jnp.zeros((8, 128), F32)
        for j in range(BLOCKS):
            got = jnp.where(lists_block == j, lane_pick(wide(load(j)), lists_lane), got)
        return got

    def collect(field, carry):
        got = list_values(lambda j: tab[pl.ds(field * 16 + j, 1), :])
        list_fixed[pl.ds(field, 4, stride=FIXED), :] = got[:4]
        return carry

    lax.fori_loop(0, FIXED, collect, 0, unroll=4)
    for b in range(4):
        rows = pl.ds(b * FIXED, FIXED)
        pltpu.make_async_remote_copy(
            list_fixed.at[rows], ghost_fixed.at[rows], fixed_send, fixed_recv,
            device_id=device(-OFFSETS[b]), device_id_type=MESH,
        ).start()

    def by_edge(fixed, lane_ref, block_ref, g_ref):
        for b in range(4):
            index = fixed[pl.ds(b * FIXED + NB, EDGES), :].astype(I32)
            lane_ref[pl.ds(b, EDGES, stride=4), :] = index & 127
            block_ref[pl.ds(b, EDGES, stride=4), :] = index >> 7
            g_ref[pl.ds(b, EDGES, stride=4), :] = fixed[pl.ds(b * FIXED + G0, EDGES), :]
            g_ref[pl.ds(24 + b, EDGES, stride=4), :] = fixed[pl.ds(b * FIXED + G1, EDGES), :]

    by_edge(list_fixed, list_lane, list_block, list_g)

    def merge_lateral():
        index = [neighbours[pl.ds(m, 1), :] for m in range(EDGES)]
        weight = [lateral[pl.ds(m, 1), :] for m in range(EDGES)]
        for m in range(1, EDGES):
            moved = index[m] == index[0]
            weight[0] = weight[0] + jnp.where(moved, weight[m], 0.0)
            for k in range(1, m):
                same = jnp.logical_and(index[m] == index[k], jnp.logical_not(moved))
                weight[k] = weight[k] + jnp.where(same, weight[m], 0.0)
                moved = jnp.logical_or(moved, same)
            weight[m] = jnp.where(moved, 0.0, weight[m])
        for m in range(EDGES):
            lateral[pl.ds(m, 1), :] = weight[m]

    def mix(n, first_row, source, column0, count_rows):
        cells = pl.ds(pl.multiple_of(n * N_COLS, N_COLS), N_COLS)
        row = lax.broadcasted_iota(I32, (count_rows, N_COLS), 0) + first_row
        matrix = jnp.zeros((count_rows, N_COLS), F32)
        for m in reversed(range(EDGES)):
            here = row == neighbours[pl.ds(m, 1), cells]
            matrix = jnp.where(here, lateral[pl.ds(m, 1), cells], matrix)
        high = matrix.astype(BF16)
        low = (matrix - high.astype(F32)).astype(BF16)
        values = source[:, pl.ds(column0, count_rows)]
        both = jnp.dot(values, high, preferred_element_type=F32)
        added = both[:ROWS] + both[ROWS:] + jnp.dot(values[:ROWS], low, preferred_element_type=F32)
        total[:, cells] = total[:, cells] + added

    def mix_own(n):
        total[:, pl.ds(pl.multiple_of(n * N_COLS, N_COLS), N_COLS)] = jnp.zeros((ROWS, N_COLS), F32)

        def step(k, carry):
            first = pl.multiple_of(k * K_ROWS, K_ROWS)
            mix(n, first, parts, first, K_ROWS)
            return carry

        lax.fori_loop(0, 2048 // K_ROWS, step, 0)

    def mix_halo(n):
        mix(n, 2048, halo_parts, 0, 512)
        sub = lax.broadcasted_iota(I32, (8, 128), 0)
        for part in range(2):
            c = n * 2 + part
            cells = pl.ds(pl.multiple_of(c * 128, 128), 128)
            weight = lateral[pl.ds(0, 1), cells]
            for m in range(1, EDGES):
                weight = weight + lateral[pl.ds(m, 1), cells]
            weight = wide(weight)
            layers = wide(count[pl.ds(c, 1), :])
            for g in range(ROWS // 8):
                rows = pl.ds(g * 8, 8)
                value = tracer[rows, cells]
                live = sub + (g * 8) % LAYERS < layers
                value = value + jnp.where(live, total[rows, cells] - weight * value, 0.0)
                profile[pl.ds(g * 128 + c, 8, stride=16), :] = value

    def select_halo():
        loads[8].wait()
        for t in range(TRACERS):
            rows = pl.ds(t * LAYERS, LAYERS)
            value = tracer[rows, :]
            high = value.astype(BF16)
            parts[rows, :] = high
            parts[pl.ds(ROWS + t * LAYERS, LAYERS), :] = (value - high.astype(F32)).astype(BF16)
        place = lax.broadcasted_iota(I32, (2048, 256), 0)
        for pair in range(2):
            lists = [halo_send[pl.ds(pair * 2 + b, 1), :] for b in range(2)]
            chosen = jnp.where(place == jnp.concatenate(lists, axis=1), 1.0, 0.0).astype(BF16)
            both = jnp.dot(parts[...], chosen, preferred_element_type=F32)
            both = both[:ROWS] + both[ROWS:]
            for b in range(2):
                halo_out[pair * 2 + b] = both[:, b * 128 : b * 128 + 128]

    def send_halo(t):
        rows = pl.ds(pl.multiple_of(t * LAYERS, LAYERS), LAYERS)
        for b in range(4):
            pltpu.make_async_remote_copy(
                halo_out.at[b, rows], halo_in.at[b, rows], halo_send_sem, halo_recv,
                device_id=device(-OFFSETS[b]), device_id_type=MESH,
            ).start()

    def layer(index):
        return pl.ds(pl.multiple_of(index * 16, 16), 16)

    def active(index):
        return (index < count[...]).astype(F32)

    def couple(index, upper):
        lower = thick_cells[layer(index + 1), :]
        return diffus_cells[layer(index), :] * 2.0 / (upper + lower) * active(index + 1)

    def vertical_gains():
        for load in loads[12:15]:
            load.wait()
        for c in range(BLOCKS):
            cells = pl.ds(c * 128, 128)
            for g in range(8):
                thick_cells[pl.ds(g * 128 + c, 8, stride=16), :] = thick[pl.ds(g * 8, 8), cells]
                size = 8 if g < 7 else 7
                diffus_cells[pl.ds(g * 128 + c, size, stride=16), :] = diffus[pl.ds(g * 8, size), cells]

        def step(i, carry):
            below, gain = carry
            index = LAYERS - 1 - i
            here = thick_cells[layer(index), :]
            above = couple(index - 1, thick_cells[layer(index - 1), :])
            inverse = 1.0 / (here + above + below - below * gain)
            gain_here[layer(index), :] = here * inverse
            gain_below[layer(index), :] = below * inverse
            gain = above * inverse
            gain_above[layer(index), :] = gain
            return above, gain

        zero = jnp.zeros((16, 128), F32)
        return lax.fori_loop(0, LAYERS - 2, step, (zero, zero))

    couple_one, gain_two = vertical_gains()
    loads[11].wait()
    merge_lateral()

    for load in loads[9:11]:
        load.wait()
    others = pl.ds(0, devices - column_size)
    pltpu.make_async_copy(arrived.at[others], arrived.at[others], ocn_recv).wait()
    stay.wait()
    square[...] = arrived[:, 0, :].T
    for slot in range(BLOCKS):
        received[slot] = square[pl.ds(slot, 8, stride=16), :]

    def remap(start):
        upper = lax.broadcasted_iota(I32, (8, 128), 0) < 4
        for slot in range(BLOCKS):
            tile = received[slot]
            other = pltpu.roll(tile, 4, 0)
            halves[slot] = jnp.where(upper, tile, other) if start == 0 else jnp.where(upper, other, tile)

        def step(pair, carry):
            cells = [pl.ds(pl.multiple_of(pair * 256 + half * 128, 128), 128) for half in range(2)]
            result = jnp.zeros((8, 128), F32)
            for k in range(4):
                index = jnp.where(upper, wide(column[pl.ds(k, 1), cells[0]]), wide(column[pl.ds(k, 1), cells[1]]))
                weight = jnp.where(
                    upper, wide(remap_weight[pl.ds(k, 1), cells[0]]), wide(remap_weight[pl.ds(k, 1), cells[1]])
                )
                lane, block = index >> 4, index & 15
                got = jnp.zeros((8, 128), F32)
                for j in range(BLOCKS):
                    got = jnp.where(block == j, lane_pick(halves[j], lane), got)
                result = result + weight * got
            flux[pl.ds(start * 16 + pair * 2, 4, stride=16), :] = result[:4]
            flux[pl.ds(start * 16 + pair * 2 + 1, 4, stride=16), :] = result[4:]
            return carry

        lax.fori_loop(0, BLOCKS // 2, step, 0, unroll=4)

    remap(4)
    tab[pl.ds(FORCE * 16, 32), :] = flux[pl.ds(64, 32), :]

    sub = lax.broadcasted_iota(I32, (8, 128), 0)
    forces = [list_values(lambda j, a=a: tab[pl.ds((FORCE + a) * 16 + j, 1), :]) for a in range(2)]
    force_out[...] = jnp.where(sub < 4, forces[0], forces[1])
    for b in range(4):
        pltpu.make_async_remote_copy(
            force_out, force_in.at[b], force_send, force_recv.at[b],
            device_id=device(-OFFSETS[b]), device_id_type=MESH,
        ).start()


    def both_halves(tile):
        return tile + pltpu.roll(tile, 4, 0)

    def send_round(s, elevation):
        for half in range(2):
            height[pl.ds(half * 8, 8), :] = elevation[half] + flux[pl.ds(96 + half * 8, 8), :]
        centre = list_values(lambda j: height[pl.ds(j, 1), :])
        first = jnp.zeros((8, 128), F32)
        second = jnp.zeros((8, 128), F32)
        for t in range(3):
            lane, block = list_lane[pl.ds(t * 8, 8), :], list_block[pl.ds(t * 8, 8), :]
            got = jnp.zeros((8, 128), F32)
            for j in range(BLOCKS):
                got = jnp.where(block == j, lane_pick(wide(height[pl.ds(j, 1), :]), lane), got)
            got = jnp.where(block < BLOCKS, got, centre)
            first = first + list_g[pl.ds(t * 8, 8), :] * (got - centre)
            second = second + list_g[pl.ds(24 + t * 8, 8), :] * (got - centre)
        first, second = both_halves(first), both_halves(second)
        sub = lax.broadcasted_iota(I32, (8, 128), 0)
        message[s, pl.ds(0, 8), :] = jnp.where(sub < 4, centre, first)
        message[s, pl.ds(8, 8), :] = second
        for ahead in (1, 0):
            for size in (2, 1, 3, 4):
                side = odd if ahead else 1 - odd
                to = device((2 * side - 1) * size)
                if size < 3:
                    pltpu.make_async_remote_copy(
                        message.at[s], near_box.at[s, 2 * (size - 1) + side], near_send, near_recv.at[s],
                        device_id=to, device_id_type=MESH,
                    ).start()
                else:
                    pltpu.make_async_remote_copy(
                        message.at[s, pl.ds(0, 8)], far_box.at[s, 2 * (size - 3) + side], far_send, far_recv.at[s],
                        device_id=to, device_id_type=MESH,
                    ).start()

    def own_sum(rows_of, centres):
        sums = [[jnp.zeros((8, 128), F32) for _ in range(2)] for _ in range(2)]
        for t in range(12):
            half, rows = t % 2, pl.ds(t * 8, 8)
            lane, block = own_lane[rows, :], own_block[rows, :]
            got = centres[half]
            for j, load in rows_of:
                got = jnp.where(block == j, lane_pick(load(), lane), got)
            apart = got - centres[half]
            for axis in range(2):
                weight = tab[pl.ds((G0 + 6 * axis) * 16 + t * 8, 8), :]
                sums[axis][half] = sums[axis][half] + weight * apart
        return sums

    def take_round(s, elevation, flow, ghost_flow, partial):
        def near(b, row):
            return wide(near_box[s, b, pl.ds(row, 1), :])

        def listed(distance, row):
            if distance == 0:
                return wide(message[s, pl.ds(row, 1), :])
            k = DISTANCES.index(distance)
            return near(k, row) if k < 4 else wide(far_box[s, k - 4, pl.ds(row, 1), :])

        which = lax.broadcasted_iota(I32, (8, 128), 0) & 3

        def by_list(load):
            out = load(0)
            for b in range(1, 4):
                out = jnp.where(which == b, load(b), out)
            return out

        centres = [height[pl.ds(half * 8, 8), :] for half in range(2)]
        rest = own_sum([(16 + b, lambda b=b: near(b, b)) for b in range(4)], centres)
        centre = by_list(lambda b: near(b, b))
        second_hand = [by_list(lambda b: listed(OFFSETS[b] + OFFSETS[j], j)) for j in range(4)]
        ghost_sums = [jnp.zeros((8, 128), F32) for _ in range(2)]
        for t in range(3):
            rows = pl.ds(t * 8, 8)
            lane, block = ghost_lane[rows, :], ghost_block[rows, :]
            got = centre
            for j in range(4):
                got = jnp.where(block == 16 + j, lane_pick(second_hand[j], lane), got)
            for axis in range(2):
                ghost_sums[axis] = ghost_sums[axis] + ghost_g[pl.ds(axis * 24 + t * 8, 8), :] * (got - centre)
        ghost_sums = [
            both_halves(ghost_sums[a]) + by_list(lambda b: near(b, 4 + 4 * a + b)) for a in range(2)
        ]

        turn = ghost_rows[pl.ds(0, 8), :]
        ghost_next = (
            ghost_flow[0] - ghost_sums[0] + turn * ghost_flow[1] + FORCE_GAIN * ghost_rows[pl.ds(8, 8), :],
            ghost_flow[1] - ghost_sums[1] - turn * ghost_flow[0] + FORCE_GAIN * ghost_rows[pl.ds(16, 8), :],
        )
        flow_next = []
        for half in range(2):
            turn = tab[pl.ds(COR * 16 + half * 8, 8), :]
            force = [tab[pl.ds((FORCE + a) * 16 + half * 8, 8), :] for a in range(2)]
            grad = [partial[a][half] + rest[a][half] for a in range(2)]
            flow_next.append(
                (
                    flow[half][0] - grad[0] + turn * flow[half][1] + FORCE_GAIN * force[0],
                    flow[half][1] - grad[1] - turn * flow[half][0] + FORCE_GAIN * force[1],
                )
            )
        for a in range(2):
            for half in range(2):
                speed[pl.ds(a * 24 + half * 8, 8), :] = flow_next[half][a]
            speed[pl.ds(a * 24 + 16, 8), :] = ghost_next[a]
        spread = [jnp.zeros((8, 128), F32) for _ in range(2)]
        for t in range(12):
            half, rows = t % 2, pl.ds(t * 8, 8)
            lane, block = own_lane[rows, :], own_block[rows, :]
            got = [jnp.zeros((8, 128), F32) for _ in range(2)]
            for j in range(20):
                here = block == j
                for a in range(2):
                    got[a] = jnp.where(here, lane_pick(wide(speed[pl.ds(a * 24 + j, 1), :]), lane), got[a])
            for a in range(2):
                weight = tab[pl.ds((G0 + 6 * a) * 16 + t * 8, 8), :]
                spread[half] = spread[half] + weight * (got[a] - flow_next[half][a])
        elevation_next = tuple(
            elevation[half] - spread[half] + FORCE_GAIN * flux[pl.ds(112 + half * 8, 8), :]
            for half in range(2)
        )
        return elevation_next, tuple(flow_next), ghost_next

    def sweep_up():
        def step(i, carry):
            index = LAYERS - 1 - i
            here, below = gain_here[layer(index), :], gain_below[layer(index), :]
            out = []
            for t in range(TRACERS):
                rows = layer(t * LAYERS + index)
                value = here * profile[rows, :] + below * carry[t]
                profile[rows, :] = value
                out.append(value)
            return tuple(out)

        zero = jnp.zeros((16, 128), F32)
        return lax.fori_loop(0, LAYERS - 2, step, (zero,) * TRACERS)

    def zero_state():
        elevation = tuple(surface[pl.ds(half * 8, 8), :] for half in range(2))
        flow = tuple(
            tuple(tab[pl.ds((VEL + a) * 16 + half * 8, 8), :] for a in range(2)) for half in range(2)
        )
        return elevation, flow

    def one_round(s, state, work):
        elevation, flow, ghost_flow = state
        centres = [height[pl.ds(half * 8, 8), :] for half in range(2)]
        own_rows = [(j, lambda j=j: wide(height[pl.ds(j, 1), :])) for j in range(16)]
        partial = own_sum(own_rows, centres)
        work()
        pltpu.make_async_copy(far_box.at[s], far_box.at[s], far_recv.at[s]).wait()
        pltpu.make_async_copy(near_box.at[s], near_box.at[s], near_recv.at[s]).wait()

        @pl.when(s == 0)
        def _():
            for b in range(4):
                pltpu.make_async_copy(force_in.at[b], force_in.at[b], force_recv.at[b]).wait()
                for a in range(2):
                    for copy in range(2):
                        row = force_in[b, pl.ds(a * 4 + b, 1), :]
                        ghost_rows[pl.ds(8 + a * 8 + copy * 4 + b, 1), :] = row

        return take_round(s, elevation, flow, ghost_flow, partial)

    elevation, flow = zero_state()
    send_round(0, elevation)
    pltpu.make_async_copy(ghost_fixed, ghost_fixed, fixed_recv).wait()
    by_edge(ghost_fixed, ghost_lane, ghost_block, ghost_g)
    for b in range(4):
        for copy in range(2):
            for row, field in ((0, COR), (24, VEL), (32, VEL + 1)):
                ghost_rows[pl.ds(row + copy * 4 + b, 1), :] = ghost_fixed[pl.ds(b * FIXED + field, 1), :]
    ghost_flow = (ghost_rows[pl.ds(24, 8), :], ghost_rows[pl.ds(32, 8), :])

    def split_halo():
        pltpu.make_async_copy(halo_in, halo_in, halo_recv).wait()
        for b in range(4):
            value = halo_in[b]
            high = value.astype(BF16)
            halo_parts[pl.ds(0, ROWS), pl.ds(b * 128, 128)] = high
            halo_parts[pl.ds(ROWS, ROWS), pl.ds(b * 128, 128)] = (value - high.astype(F32)).astype(BF16)

    def sweep_down(index, carry):
        above = gain_above[layer(index), :]
        share = above * carry[0]
        gain_above[layer(index), :] = share
        out = []
        for t in range(TRACERS):
            rows = layer(t * LAYERS + index)
            value = profile[rows, :] + above * carry[1 + t]
            profile[rows, :] = value
            out.append(value)
        return (share, *out)

    def place_out(c, carry):
        cells = pl.ds(pl.multiple_of(c * 128, 128), 128)
        deep = lax.broadcasted_iota(I32, (8, 128), 0) > 1
        for g in range(ROWS // 8):
            value = profile[pl.ds(g * 128 + c, 8, stride=16), :]
            if g % 8 == 0:
                value = jnp.where(deep, value, 0.0)
            total[pl.ds(g * 8, 8), cells] = value
        for g in range(LAYERS // 8):
            thick[pl.ds(g * 8, 8), cells] = gain_above[pl.ds(g * 128 + c, 8, stride=16), :]
        return carry

    stores = (
        pltpu.make_async_copy(total, rest_hbm, store_sem.at[0]),
        pltpu.make_async_copy(thick, share_hbm, store_sem.at[1]),
    )

    def solve_below():
        values = sweep_up()
        for t in range(TRACERS):
            tops[pl.ds(t * 16, 16), :] = values[t]
        zero, one = jnp.zeros((16, 128), F32), jnp.ones((16, 128), F32)
        gain_above[layer(0), :] = zero
        gain_above[layer(1), :] = one
        lax.fori_loop(2, LAYERS, sweep_down, (one,) + (zero,) * TRACERS)
        lax.fori_loop(0, BLOCKS, place_out, 0)
        for store in stores:
            store.start()

    def tracer_work(s):
        @pl.when(s == 0)
        def _():
            select_halo()

        @pl.when(s < 4)
        def _():
            send_halo(s)

        @pl.when(jnp.logical_and(s >= 1, s < 5))
        def _():
            def step(i, carry):
                mix_own(2 * (s - 1) + i)
                return carry

            lax.fori_loop(0, 2, step, 0)

        @pl.when(s == 5)
        def _():
            split_halo()
            remap(0)

        @pl.when(jnp.logical_and(s >= 5, s < 7))
        def _():
            def step(i, carry):
                mix_halo(4 * (s - 5) + i)
                return carry

            lax.fori_loop(0, 4, step, 0)

        @pl.when(s == 7)
        def _():
            solve_below()

    def subcycle(s, state):
        state = one_round(s, state, lambda: tracer_work(s))

        @pl.when(s < SUBCYCLES - 1)
        def _():
            send_round(s + 1, state[0])

        return state

    elevation, flow, ghost_flow = lax.fori_loop(0, SUBCYCLES, subcycle, (elevation, flow, ghost_flow))

    for half in range(2):
        final_surface[pl.ds(half * 8, 8), :] = elevation[half]
    for c in range(BLOCKS):
        final_velocity[0:1, pl.ds(c * 128, 128)] = speed[pl.ds(c, 1), :]
        final_velocity[1:2, pl.ds(c * 128, 128)] = speed[pl.ds(24 + c, 1), :]

    top = thick_cells[layer(0), :] + jnp.tanh(final_surface[...])
    second = thick_cells[layer(1), :]
    couple_zero = couple(0, top)
    inverse_one = 1.0 / (second + couple_zero + couple_one - couple_one * gain_two)
    gain_one = couple_zero * inverse_one
    inverse_zero = 1.0 / (top + couple_zero - couple_zero * gain_one)
    for t in range(TRACERS):
        rows_zero, rows_one = layer(t * LAYERS), layer(t * LAYERS + 1)
        value_one = (second * profile[rows_one, :] + couple_one * tops[pl.ds(t * 16, 16), :]) * inverse_one
        right = top * profile[rows_zero, :] + FLUX_GAIN * flux[pl.ds(t * 16, 16), :]
        value_zero = (right + couple_zero * value_one) * inverse_zero
        square[pl.ds(t * 16, 16), :] = value_zero
        square[pl.ds(64 + t * 16, 16), :] = value_one + gain_one * value_zero
    for c in range(BLOCKS):
        heads[:, pl.ds(c * 128, 128)] = square[pl.ds(c, 8, stride=16), :]

    for store in stores:
        store.wait()
    pltpu.make_async_copy(near_box, near_box, near_send).wait()
    pltpu.make_async_copy(far_box, far_box, far_send).wait()
    pltpu.make_async_copy(list_fixed, list_fixed, fixed_send).wait()
    pltpu.make_async_copy(force_in, force_in, force_send).wait()
    pltpu.make_async_copy(halo_out, halo_out, halo_send_sem).wait()
    pltpu.make_async_copy(gathered, gathered, col_send).wait()
    pltpu.make_async_copy(arrived.at[others], arrived.at[others], ocn_send).wait()


def finish_kernel(
    rest_hbm, share_hbm, heads_hbm, surface_hbm, flow_hbm, mixed_hbm, surface_out, flow_out,
    rest, share, heads, load_sem, store_sem,
):
    loads = [
        pltpu.make_async_copy(share_hbm, share, load_sem.at[0]),
        pltpu.make_async_copy(heads_hbm, heads, load_sem.at[1]),
    ]
    stores = [
        pltpu.make_async_copy(surface_hbm, surface_out, store_sem.at[0]),
        pltpu.make_async_copy(flow_hbm, flow_out, store_sem.at[1]),
    ]
    pieces = [pl.ds(start, PIECE) for start in range(0, ROWS, PIECE)]
    for i, rows in enumerate(pieces):
        loads.append(pltpu.make_async_copy(rest_hbm.at[rows], rest.at[rows], load_sem.at[2 + i]))
        stores.append(pltpu.make_async_copy(rest.at[rows], mixed_hbm.at[rows], store_sem.at[2 + i]))
    for copy in loads + stores[:2]:
        copy.start()
    loads[0].wait()
    loads[1].wait()
    sub = lax.broadcasted_iota(I32, (8, 2048), 0)
    for i in range(len(pieces)):
        loads[2 + i].wait()
        t = i * PIECE // LAYERS
        head = jnp.broadcast_to(heads[pl.ds(4 + t, 1), :], (8, 2048))
        for first in range(i * PIECE, (i + 1) * PIECE, 8):
            rows = pl.ds(first, 8)
            value = rest[rows, :] + share[pl.ds(first % LAYERS, 8), :] * head
            if first % LAYERS == 0:
                value = jnp.where(sub == 0, jnp.broadcast_to(heads[pl.ds(t, 1), :], (8, 2048)), value)
            rest[rows, :] = value
        stores[2 + i].start()
    for store in stores:
        store.wait()


def finish(*operands):
    hbm = pl.BlockSpec(memory_space=pl.ANY)
    return pl.pallas_call(
        finish_kernel,
        name="finish",
        out_shape=(
            jax.ShapeDtypeStruct((ROWS, 2048), F32),
            jax.ShapeDtypeStruct((16, 128), F32),
            jax.ShapeDtypeStruct((2, 2048), F32),
        ),
        in_specs=[hbm] * 5,
        out_specs=(hbm,) * 3,
        scratch_shapes=[
            pltpu.VMEM((ROWS, 2048), F32),
            pltpu.VMEM((LAYERS, 2048), F32),
            pltpu.VMEM((8, 2048), F32),
            pltpu.SemaphoreType.DMA((2 + ROWS // PIECE,)),
            pltpu.SemaphoreType.DMA((2 + ROWS // PIECE,)),
        ],
        compiler_params=pltpu.CompilerParams(vmem_limit_bytes=60 << 20),
    )(*operands)


def ocean(ocn_size, col_size, *operands):
    vmem = pl.BlockSpec(memory_space=pltpu.VMEM)
    hbm = pl.BlockSpec(memory_space=pl.ANY)

    def kernel(*refs):
        ocean_kernel(ocn_size, col_size, *refs)

    scratch = [
        pltpu.VMEM((8, 2048), F32),
        pltpu.VMEM((16, 128), I32),
        pltpu.VMEM((4, 2048), I32),
        pltpu.VMEM((4, 2048), F32),
        pltpu.VMEM((1, 4, 128), I32),
        pltpu.VMEM((EDGES, 2048), I32),
        pltpu.VMEM((EDGES, 2, 2048), F32),
        pltpu.VMEM((16, 128), F32),
        pltpu.VMEM((16, 128), F32),
        pltpu.VMEM((2, 2048), F32),
        pltpu.VMEM((EDGES, 2048), F32),
        pltpu.VMEM((16, 128), I32),
        pltpu.VMEM((LAYERS, 2048), F32),
        pltpu.VMEM((LAYERS - 1, 2048), F32),
        pltpu.VMEM((ROWS, 2048), F32),
        pltpu.VMEM((FIXED * 16, 128), F32),
        pltpu.VMEM((128, 128), F32),
        pltpu.VMEM((ocn_size // 2, 2 * col_size, 1, 128), F32),
        pltpu.VMEM((2 * col_size, ocn_size // 2, 1, 128), F32),
        pltpu.VMEM((ocn_size * col_size, 1, 128), F32),
        pltpu.VMEM((16, 8, 128), F32),
        pltpu.VMEM((16, 8, 128), F32),
        pltpu.VMEM((128, 128), F32),
        pltpu.VMEM((4 * FIXED, 128), F32),
        pltpu.VMEM((4 * FIXED, 128), F32),
        pltpu.VMEM((8, 128), F32),
        pltpu.VMEM((4, 8, 128), F32),
        pltpu.VMEM((96, 128), I32),
        pltpu.VMEM((96, 128), I32),
        pltpu.VMEM((24, 128), I32),
        pltpu.VMEM((24, 128), I32),
        pltpu.VMEM((48, 128), F32),
        pltpu.VMEM((24, 128), I32),
        pltpu.VMEM((24, 128), I32),
        pltpu.VMEM((48, 128), F32),
        pltpu.VMEM((16, 128), F32),
        pltpu.VMEM((48, 128), F32),
        pltpu.VMEM((40, 128), F32),
        pltpu.VMEM((SUBCYCLES, 16, 128), F32),
        pltpu.VMEM((SUBCYCLES, 4, 16, 128), F32),
        pltpu.VMEM((SUBCYCLES, 4, 8, 128), F32),
        pltpu.VMEM((4, ROWS, 128), F32),
        pltpu.VMEM((4, ROWS, 128), F32),
        pltpu.VMEM((2 * ROWS, 2048), BF16),
        pltpu.VMEM((2 * ROWS, 512), BF16),
        pltpu.VMEM((ROWS, 2048), F32),
        pltpu.VMEM((ROWS * 16, 128), F32),
        pltpu.VMEM((LAYERS * 16, 128), F32),
        pltpu.VMEM((LAYERS * 16, 128), F32),
        pltpu.VMEM((LAYERS * 16, 128), F32),
        pltpu.VMEM((LAYERS * 16, 128), F32),
        pltpu.VMEM((LAYERS * 16, 128), F32),
        pltpu.VMEM((TRACERS * 16, 128), F32),
        pltpu.SemaphoreType.DMA((15,)),
        pltpu.SemaphoreType.DMA((2,)),
        pltpu.SemaphoreType.DMA,
        pltpu.SemaphoreType.DMA,
        pltpu.SemaphoreType.DMA,
        pltpu.SemaphoreType.DMA,
        pltpu.SemaphoreType.DMA,
        pltpu.SemaphoreType.DMA,
        pltpu.SemaphoreType.DMA,
        pltpu.SemaphoreType.DMA,
        pltpu.SemaphoreType.DMA,
        pltpu.SemaphoreType.DMA((4,)),
        pltpu.SemaphoreType.DMA,
        pltpu.SemaphoreType.DMA,
        pltpu.SemaphoreType.DMA,
        pltpu.SemaphoreType.DMA((SUBCYCLES,)),
        pltpu.SemaphoreType.DMA,
        pltpu.SemaphoreType.DMA((SUBCYCLES,)),
    ]
    return pl.pallas_call(
        kernel,
        name="ocean",
        out_shape=(
            jax.ShapeDtypeStruct((ROWS, 2048), F32),
            jax.ShapeDtypeStruct((LAYERS, 2048), F32),
            jax.ShapeDtypeStruct((8, 2048), F32),
            jax.ShapeDtypeStruct((16, 128), F32),
            jax.ShapeDtypeStruct((2, 2048), F32),
        ),
        in_specs=[hbm] * 15,
        out_specs=(hbm, hbm, vmem, vmem, vmem),
        scratch_shapes=scratch,
        compiler_params=pltpu.CompilerParams(
            collective_id=0, has_side_effects=True, vmem_limit_bytes=60 << 20
        ),
    )(*operands)


def solution(mesh):
    ocn_size, col_size = mesh.shape["ocn"], mesh.shape["col"]

    def per_device(
        air_flux,
        send_index,
        remap_column,
        remap_weight,
        halo_send,
        neighbours,
        gradient_weight,
        coriolis,
        sea_surface,
        velocity,
        lateral_weight,
        layer_count,
        thickness,
        diffusivity,
        tracers,
    ):
        solved = ocean(
            ocn_size,
            col_size,
            air_flux,
            send_index[0].T,
            remap_column,
            remap_weight,
            halo_send,
            neighbours,
            jnp.swapaxes(gradient_weight, 0, 1),
            coriolis.reshape(16, 128),
            sea_surface.reshape(16, 128),
            velocity,
            lateral_weight,
            layer_count.reshape(16, 128),
            thickness,
            diffusivity,
            tracers.reshape(ROWS, 2048),
        )
        mixed, elevation, flow = finish(*solved)
        return mixed.reshape(TRACERS, LAYERS, 2048), elevation.reshape(2048), flow

    both = ("ocn", "col")
    placed = (
        P(None, both),
        P(both, None, None),
        P(None, both),
        P(None, both),
        P(both, None, None),
        P(None, both),
        P(None, None, both),
        P(both),
        P(both),
        P(None, both),
        P(None, both),
        P(both),
        P(None, both),
        P(None, both),
        P(None, None, both),
    )
    return jax.shard_map(
        per_device,
        mesh=mesh,
        in_specs=placed,
        out_specs=(P(None, None, both), P(both), P(None, both)),
        check_vma=False,
    )
```

```python
import jax
import jax.numpy as jnp
from jax import lax
from jax.experimental import pallas as pl
from jax.experimental.pallas import tpu as pltpu
from jax.sharding import PartitionSpec as P

F32 = jnp.float32
BF16 = jnp.bfloat16
I32 = jnp.int32
MESH = pl.DeviceIdType.MESH

SUBCYCLES = 8
LAYERS = 64
TRACERS = 4
ROWS = TRACERS * LAYERS
EDGES = 6
BLOCKS = 16
OFFSETS = (1, -1, 2, -2)
DISTANCES = (1, -1, 2, -2, 3, -3, 4, -4)
FLUX_GAIN = 2.0
FORCE_GAIN = 0.05

NB, G0, G1, COR, VEL, FORCE, FIXED = 0, 6, 12, 18, 19, 21, 24
N_COLS = 256
K_ROWS = 1024
PIECE = 32


def wide(row):
    return jnp.broadcast_to(row, (8, 128))


def lane_pick(source, lane):
    return jnp.take_along_axis(source, lane, axis=1, mode="promise_in_bounds")


def ocean_kernel(
    ocn_size,
    col_size,
    air_hbm,
    send_hbm,
    column_hbm,
    remap_hbm,
    halo_send_hbm,
    neighbours_hbm,
    gradient_hbm,
    coriolis_hbm,
    surface_hbm,
    velocity_hbm,
    lateral_hbm,
    count_hbm,
    thick_hbm,
    diffusivity_hbm,
    tracer_hbm,
    rest_hbm,
    share_hbm,
    heads,
    final_surface,
    final_velocity,
    air,
    send_index,
    column,
    remap_weight,
    halo_lists,
    neighbours,
    gradient,
    coriolis,
    surface,
    velocity,
    lateral,
    count,
    thick,
    diffus,
    tracer,
    tab,
    square,
    outgoing,
    passing,
    arrived,
    received,
    halves,
    flux,
    list_fixed,
    ghost_fixed,
    force_out,
    force_in,
    own_lane,
    own_block,
    list_lane,
    list_block,
    list_g,
    ghost_lane,
    ghost_block,
    ghost_g,
    height,
    speed,
    ghost_rows,
    message,
    near_box,
    far_box,
    halo_out,
    halo_in,
    parts,
    halo_parts,
    total,
    profile,
    thick_cells,
    diffus_cells,
    gain_here,
    gain_below,
    gain_above,
    tops,
    load_sem,
    store_sem,
    col_send,
    col_recv,
    col_own,
    ocn_send,
    ocn_recv,
    ocn_own,
    fixed_send,
    fixed_recv,
    force_send,
    force_recv,
    halo_send_sem,
    halo_recv,
    near_send,
    near_recv,
    far_send,
    far_recv,
):
    devices = ocn_size * col_size
    ocn, col = lax.axis_index("ocn"), lax.axis_index("col")
    me = ocn * col_size + col
    odd = lax.rem(ocn, 2)

    def device(distance):
        target = lax.rem(me + (distance + devices), devices)
        return (target // col_size, lax.rem(target, col_size))

    column_size = 2 * col_size
    chips = ocn_size // 2
    chip, place_in_column = ocn // 2, odd * col_size + col

    def in_column(step):
        to = lax.rem(place_in_column + step, column_size)
        return to, (chip * 2 + to // col_size, lax.rem(to, col_size))

    def across(step):
        to = lax.rem(chip + step, chips)
        return to, (to * 2 + odd, col)

    sources = (
        air_hbm, send_hbm, halo_send_hbm, neighbours_hbm, gradient_hbm, coriolis_hbm, surface_hbm, velocity_hbm,
        tracer_hbm, column_hbm, remap_hbm, lateral_hbm, count_hbm, thick_hbm, diffusivity_hbm,
    )
    targets = (
        air, send_index, halo_lists, neighbours, gradient, coriolis, surface, velocity,
        tracer, column, remap_weight, lateral, count, thick, diffus,
    )
    loads = [
        pltpu.make_async_copy(source, target, load_sem.at[i])
        for i, (source, target) in enumerate(zip(sources, targets))
    ]
    for load in loads[:2]:
        load.start()

    barrier = pltpu.get_barrier_semaphore()
    for step in range(1, chips):
        pl.semaphore_signal(barrier, inc=1, device_id=across(step)[1], device_id_type=MESH)
    for distance in DISTANCES:
        pl.semaphore_signal(barrier, inc=1, device_id=device(distance), device_id_type=MESH)
    for step in range(1, column_size):
        pl.semaphore_signal(barrier, inc=1, device_id=in_column(step)[1], device_id_type=MESH)
    for load in loads[2:]:
        load.start()

    loads[0].wait()
    loads[1].wait()
    for slot in range(BLOCKS):
        index = wide(send_index[pl.ds(slot, 1), :])
        lane, block = index & 127, index >> 7
        got = jnp.zeros((8, 128), F32)
        for j in range(BLOCKS):
            got = jnp.where(block == j, lane_pick(air[:, pl.ds(j * 128, 128)], lane), got)
        square[pl.ds(slot, 8, stride=16), :] = got
    turned = square[...].T
    for target in range(ocn_size * col_size):
        outgoing[target // column_size, target % column_size, :, :] = turned[target : target + 1]
    pl.semaphore_wait(barrier, len(DISTANCES) + column_size - 1 + chips - 1)
    for i in range(column_size - 1):
        to, target = in_column(1 + (i + 1) % (column_size - 1))
        pltpu.make_async_remote_copy(
            outgoing.at[:, to], passing.at[place_in_column], col_send, col_recv,
            device_id=target, device_id_type=MESH,
        ).start()
    stay = pltpu.make_async_copy(outgoing.at[:, place_in_column], passing.at[place_in_column], col_own)
    stay.start()

    for load in loads[2:8]:
        load.wait()
    halo_send = halo_lists.at[0]

    for c in range(BLOCKS):
        cells = pl.ds(c * 128, 128)
        tab[pl.ds(NB * 16 + c, EDGES, stride=16), :] = neighbours[:, cells].astype(F32)
        for m in range(EDGES):
            tab[pl.ds((G0 + m) * 16 + c, 2, stride=16 * EDGES), :] = gradient[m, :, cells]
        tab[pl.ds(VEL * 16 + c, 2, stride=16), :] = velocity[:, cells]
    tab[pl.ds(COR * 16, 16), :] = coriolis[...]
    tab[pl.ds(FORCE * 16, 48), :] = jnp.zeros((48, 128), F32)
    for t in range(12):
        index = tab[pl.ds(t * 8, 8), :].astype(I32)
        own_lane[pl.ds(t * 8, 8), :] = index & 127
        own_block[pl.ds(t * 8, 8), :] = index >> 7

    gathered = passing.at[pl.ds(0, column_size - 1)]
    pltpu.make_async_copy(gathered, gathered, col_recv).wait()
    stay.wait()
    landing = arrived.at[pl.ds(chip * column_size, column_size)]
    for i in range(chips - 1):
        to, target = across(1 + (i + chips // 2 - 3) % (chips - 1))
        pltpu.make_async_remote_copy(
            passing.at[:, to], landing, ocn_send, ocn_recv, device_id=target, device_id_type=MESH
        ).start()
    stay = pltpu.make_async_copy(passing.at[:, chip], landing, ocn_own)
    stay.start()

    lists = jnp.concatenate([halo_send[...]] * 2, axis=0)
    lists_lane, lists_block = lists & 127, lists >> 7

    def list_values(load):
        got = jnp.zeros((8, 128), F32)
        for j in range(BLOCKS):
            got = jnp.where(lists_block == j, lane_pick(wide(load(j)), lists_lane), got)
        return got

    def collect(field, carry):
        got = list_values(lambda j: tab[pl.ds(field * 16 + j, 1), :])
        list_fixed[pl.ds(field, 4, stride=FIXED), :] = got[:4]
        return carry

    lax.fori_loop(0, FIXED, collect, 0, unroll=4)
    for b in range(4):
        rows = pl.ds(b * FIXED, FIXED)
        pltpu.make_async_remote_copy(
            list_fixed.at[rows], ghost_fixed.at[rows], fixed_send, fixed_recv,
            device_id=device(-OFFSETS[b]), device_id_type=MESH,
        ).start()

    def by_edge(fixed, lane_ref, block_ref, g_ref):
        for b in range(4):
            index = fixed[pl.ds(b * FIXED + NB, EDGES), :].astype(I32)
            lane_ref[pl.ds(b, EDGES, stride=4), :] = index & 127
            block_ref[pl.ds(b, EDGES, stride=4), :] = index >> 7
            g_ref[pl.ds(b, EDGES, stride=4), :] = fixed[pl.ds(b * FIXED + G0, EDGES), :]
            g_ref[pl.ds(24 + b, EDGES, stride=4), :] = fixed[pl.ds(b * FIXED + G1, EDGES), :]

    by_edge(list_fixed, list_lane, list_block, list_g)

    def merge_lateral():
        index = [neighbours[pl.ds(m, 1), :] for m in range(EDGES)]
        weight = [lateral[pl.ds(m, 1), :] for m in range(EDGES)]
        for m in range(1, EDGES):
            moved = index[m] == index[0]
            weight[0] = weight[0] + jnp.where(moved, weight[m], 0.0)
            for k in range(1, m):
                same = jnp.logical_and(index[m] == index[k], jnp.logical_not(moved))
                weight[k] = weight[k] + jnp.where(same, weight[m], 0.0)
                moved = jnp.logical_or(moved, same)
            weight[m] = jnp.where(moved, 0.0, weight[m])
        for m in range(EDGES):
            lateral[pl.ds(m, 1), :] = weight[m]

    def mix(n, first_row, source, column0, count_rows):
        cells = pl.ds(pl.multiple_of(n * N_COLS, N_COLS), N_COLS)
        row = lax.broadcasted_iota(I32, (count_rows, N_COLS), 0) + first_row
        matrix = jnp.zeros((count_rows, N_COLS), F32)
        for m in reversed(range(EDGES)):
            here = row == neighbours[pl.ds(m, 1), cells]
            matrix = jnp.where(here, lateral[pl.ds(m, 1), cells], matrix)
        high = matrix.astype(BF16)
        low = (matrix - high.astype(F32)).astype(BF16)
        values = source[:, pl.ds(column0, count_rows)]
        both = jnp.dot(values, high, preferred_element_type=F32)
        added = both[:ROWS] + both[ROWS:] + jnp.dot(values[:ROWS], low, preferred_element_type=F32)
        total[:, cells] = total[:, cells] + added

    def mix_own(n):
        total[:, pl.ds(pl.multiple_of(n * N_COLS, N_COLS), N_COLS)] = jnp.zeros((ROWS, N_COLS), F32)

        def step(k, carry):
            first = pl.multiple_of(k * K_ROWS, K_ROWS)
            mix(n, first, parts, first, K_ROWS)
            return carry

        lax.fori_loop(0, 2048 // K_ROWS, step, 0)

    def mix_halo(n):
        mix(n, 2048, halo_parts, 0, 512)
        sub = lax.broadcasted_iota(I32, (8, 128), 0)
        for part in range(2):
            c = n * 2 + part
            cells = pl.ds(pl.multiple_of(c * 128, 128), 128)
            weight = lateral[pl.ds(0, 1), cells]
            for m in range(1, EDGES):
                weight = weight + lateral[pl.ds(m, 1), cells]
            weight = wide(weight)
            layers = wide(count[pl.ds(c, 1), :])
            for g in range(ROWS // 8):
                rows = pl.ds(g * 8, 8)
                value = tracer[rows, cells]
                live = sub + (g * 8) % LAYERS < layers
                value = value + jnp.where(live, total[rows, cells] - weight * value, 0.0)
                profile[pl.ds(g * 128 + c, 8, stride=16), :] = value

    def select_halo():
        loads[8].wait()
        for t in range(TRACERS):
            rows = pl.ds(t * LAYERS, LAYERS)
            value = tracer[rows, :]
            high = value.astype(BF16)
            parts[rows, :] = high
            parts[pl.ds(ROWS + t * LAYERS, LAYERS), :] = (value - high.astype(F32)).astype(BF16)
        place = lax.broadcasted_iota(I32, (2048, 256), 0)
        for pair in range(2):
            lists = [halo_send[pl.ds(pair * 2 + b, 1), :] for b in range(2)]
            chosen = jnp.where(place == jnp.concatenate(lists, axis=1), 1.0, 0.0).astype(BF16)
            both = jnp.dot(parts[...], chosen, preferred_element_type=F32)
            both = both[:ROWS] + both[ROWS:]
            for b in range(2):
                halo_out[pair * 2 + b] = both[:, b * 128 : b * 128 + 128]

    def send_halo(t):
        rows = pl.ds(pl.multiple_of(t * LAYERS, LAYERS), LAYERS)
        for b in range(4):
            pltpu.make_async_remote_copy(
                halo_out.at[b, rows], halo_in.at[b, rows], halo_send_sem, halo_recv,
                device_id=device(-OFFSETS[b]), device_id_type=MESH,
            ).start()

    def layer(index):
        return pl.ds(pl.multiple_of(index * 16, 16), 16)

    def active(index):
        return (index < count[...]).astype(F32)

    def couple(index, upper):
        lower = thick_cells[layer(index + 1), :]
        return diffus_cells[layer(index), :] * 2.0 / (upper + lower) * active(index + 1)

    def vertical_gains():
        for load in loads[12:15]:
            load.wait()
        for c in range(BLOCKS):
            cells = pl.ds(c * 128, 128)
            for g in range(8):
                thick_cells[pl.ds(g * 128 + c, 8, stride=16), :] = thick[pl.ds(g * 8, 8), cells]
                size = 8 if g < 7 else 7
                diffus_cells[pl.ds(g * 128 + c, size, stride=16), :] = diffus[pl.ds(g * 8, size), cells]

        def step(i, carry):
            below, gain = carry
            index = LAYERS - 1 - i
            here = thick_cells[layer(index), :]
            above = couple(index - 1, thick_cells[layer(index - 1), :])
            inverse = 1.0 / (here + above + below - below * gain)
            gain_here[layer(index), :] = here * inverse
            gain_below[layer(index), :] = below * inverse
            gain = above * inverse
            gain_above[layer(index), :] = gain
            return above, gain

        zero = jnp.zeros((16, 128), F32)
        return lax.fori_loop(0, LAYERS - 2, step, (zero, zero))

    couple_one, gain_two = vertical_gains()
    loads[11].wait()
    merge_lateral()

    for load in loads[9:11]:
        load.wait()
    others = pl.ds(0, devices - column_size)
    pltpu.make_async_copy(arrived.at[others], arrived.at[others], ocn_recv).wait()
    stay.wait()
    square[...] = arrived[:, 0, :].T
    for slot in range(BLOCKS):
        received[slot] = square[pl.ds(slot, 8, stride=16), :]

    def remap(start):
        upper = lax.broadcasted_iota(I32, (8, 128), 0) < 4
        for slot in range(BLOCKS):
            tile = received[slot]
            other = pltpu.roll(tile, 4, 0)
            halves[slot] = jnp.where(upper, tile, other) if start == 0 else jnp.where(upper, other, tile)

        def step(pair, carry):
            cells = [pl.ds(pl.multiple_of(pair * 256 + half * 128, 128), 128) for half in range(2)]
            result = jnp.zeros((8, 128), F32)
            for k in range(4):
                index = jnp.where(upper, wide(column[pl.ds(k, 1), cells[0]]), wide(column[pl.ds(k, 1), cells[1]]))
                weight = jnp.where(
                    upper, wide(remap_weight[pl.ds(k, 1), cells[0]]), wide(remap_weight[pl.ds(k, 1), cells[1]])
                )
                lane, block = index >> 4, index & 15
                got = jnp.zeros((8, 128), F32)
                for j in range(BLOCKS):
                    got = jnp.where(block == j, lane_pick(halves[j], lane), got)
                result = result + weight * got
            flux[pl.ds(start * 16 + pair * 2, 4, stride=16), :] = result[:4]
            flux[pl.ds(start * 16 + pair * 2 + 1, 4, stride=16), :] = result[4:]
            return carry

        lax.fori_loop(0, BLOCKS // 2, step, 0, unroll=4)

    remap(4)
    tab[pl.ds(FORCE * 16, 32), :] = flux[pl.ds(64, 32), :]

    sub = lax.broadcasted_iota(I32, (8, 128), 0)
    forces = [list_values(lambda j, a=a: tab[pl.ds((FORCE + a) * 16 + j, 1), :]) for a in range(2)]
    force_out[...] = jnp.where(sub < 4, forces[0], forces[1])
    for b in range(4):
        pltpu.make_async_remote_copy(
            force_out, force_in.at[b], force_send, force_recv.at[b],
            device_id=device(-OFFSETS[b]), device_id_type=MESH,
        ).start()


    def both_halves(tile):
        return tile + pltpu.roll(tile, 4, 0)

    def send_round(s, elevation):
        for half in range(2):
            height[pl.ds(half * 8, 8), :] = elevation[half] + flux[pl.ds(96 + half * 8, 8), :]
        centre = list_values(lambda j: height[pl.ds(j, 1), :])
        first = jnp.zeros((8, 128), F32)
        second = jnp.zeros((8, 128), F32)
        for t in range(3):
            lane, block = list_lane[pl.ds(t * 8, 8), :], list_block[pl.ds(t * 8, 8), :]
            got = jnp.zeros((8, 128), F32)
            for j in range(BLOCKS):
                got = jnp.where(block == j, lane_pick(wide(height[pl.ds(j, 1), :]), lane), got)
            got = jnp.where(block < BLOCKS, got, centre)
            first = first + list_g[pl.ds(t * 8, 8), :] * (got - centre)
            second = second + list_g[pl.ds(24 + t * 8, 8), :] * (got - centre)
        first = both_halves(first)
        second = pltpu.roll(second, 1, 0) + pltpu.roll(second, 5, 0)
        sub = lax.broadcasted_iota(I32, (8, 128), 0)
        for b in range(4):
            message[s, b, :, :] = jnp.where(sub < 4, centre, jnp.where(sub == 4 + b, first, second))
        for ahead in (1, 0):
            for size in (2, 1, 3, 4):
                side = odd if ahead else 1 - odd
                to = device((2 * side - 1) * size)
                if size < 3:
                    pltpu.make_async_remote_copy(
                        message.at[s, 2 * (size - 1) + side], near_box.at[s, 2 * (size - 1) + side], near_send, near_recv.at[s],
                        device_id=to, device_id_type=MESH,
                    ).start()
                else:
                    pltpu.make_async_remote_copy(
                        message.at[s, 0], far_box.at[s, 2 * (size - 3) + side], far_send, far_recv.at[s],
                        device_id=to, device_id_type=MESH,
                    ).start()

    def own_sum(rows_of, centres):
        sums = [[jnp.zeros((8, 128), F32) for _ in range(2)] for _ in range(2)]
        for t in range(12):
            half, rows = t % 2, pl.ds(t * 8, 8)
            lane, block = own_lane[rows, :], own_block[rows, :]
            got = centres[half]
            for j, load in rows_of:
                got = jnp.where(block == j, lane_pick(load(), lane), got)
            apart = got - centres[half]
            for axis in range(2):
                weight = tab[pl.ds((G0 + 6 * axis) * 16 + t * 8, 8), :]
                sums[axis][half] = sums[axis][half] + weight * apart
        return sums

    def take_round(s, elevation, flow, ghost_flow, partial):
        def near(b, row):
            return wide(near_box[s, b, pl.ds(row, 1), :])

        def listed(distance, row):
            if distance == 0:
                return wide(message[s, 0, pl.ds(row, 1), :])
            k = DISTANCES.index(distance)
            return near(k, row) if k < 4 else wide(far_box[s, k - 4, pl.ds(row, 1), :])

        which = lax.broadcasted_iota(I32, (8, 128), 0) & 3

        def by_list(load):
            out = load(0)
            for b in range(1, 4):
                out = jnp.where(which == b, load(b), out)
            return out

        centres = [height[pl.ds(half * 8, 8), :] for half in range(2)]
        rest = own_sum([(16 + b, lambda b=b: near(b, b)) for b in range(4)], centres)
        centre = by_list(lambda b: near(b, b))
        second_hand = [by_list(lambda b: listed(OFFSETS[b] + OFFSETS[j], j)) for j in range(4)]
        ghost_sums = [jnp.zeros((8, 128), F32) for _ in range(2)]
        for t in range(3):
            rows = pl.ds(t * 8, 8)
            lane, block = ghost_lane[rows, :], ghost_block[rows, :]
            got = centre
            for j in range(4):
                got = jnp.where(block == 16 + j, lane_pick(second_hand[j], lane), got)
            for axis in range(2):
                ghost_sums[axis] = ghost_sums[axis] + ghost_g[pl.ds(axis * 24 + t * 8, 8), :] * (got - centre)
        ghost_sums = [
            both_halves(ghost_sums[a]) + by_list(lambda b: near(b, 4 + (b + a) % 4)) for a in range(2)
        ]

        turn = ghost_rows[pl.ds(0, 8), :]
        ghost_next = (
            ghost_flow[0] - ghost_sums[0] + turn * ghost_flow[1] + FORCE_GAIN * ghost_rows[pl.ds(8, 8), :],
            ghost_flow[1] - ghost_sums[1] - turn * ghost_flow[0] + FORCE_GAIN * ghost_rows[pl.ds(16, 8), :],
        )
        flow_next = []
        for half in range(2):
            turn = tab[pl.ds(COR * 16 + half * 8, 8), :]
            force = [tab[pl.ds((FORCE + a) * 16 + half * 8, 8), :] for a in range(2)]
            grad = [partial[a][half] + rest[a][half] for a in range(2)]
            flow_next.append(
                (
                    flow[half][0] - grad[0] + turn * flow[half][1] + FORCE_GAIN * force[0],
                    flow[half][1] - grad[1] - turn * flow[half][0] + FORCE_GAIN * force[1],
                )
            )
        for a in range(2):
            for half in range(2):
                speed[pl.ds(a * 24 + half * 8, 8), :] = flow_next[half][a]
            speed[pl.ds(a * 24 + 16, 8), :] = ghost_next[a]
        spread = [jnp.zeros((8, 128), F32) for _ in range(2)]
        for t in range(12):
            half, rows = t % 2, pl.ds(t * 8, 8)
            lane, block = own_lane[rows, :], own_block[rows, :]
            got = [jnp.zeros((8, 128), F32) for _ in range(2)]
            for j in range(20):
                here = block == j
                for a in range(2):
                    got[a] = jnp.where(here, lane_pick(wide(speed[pl.ds(a * 24 + j, 1), :]), lane), got[a])
            for a in range(2):
                weight = tab[pl.ds((G0 + 6 * a) * 16 + t * 8, 8), :]
                spread[half] = spread[half] + weight * (got[a] - flow_next[half][a])
        elevation_next = tuple(
            elevation[half] - spread[half] + FORCE_GAIN * flux[pl.ds(112 + half * 8, 8), :]
            for half in range(2)
        )
        return elevation_next, tuple(flow_next), ghost_next

    def sweep_up():
        def step(i, carry):
            index = LAYERS - 1 - i
            here, below = gain_here[layer(index), :], gain_below[layer(index), :]
            out = []
            for t in range(TRACERS):
                rows = layer(t * LAYERS + index)
                value = here * profile[rows, :] + below * carry[t]
                profile[rows, :] = value
                out.append(value)
            return tuple(out)

        zero = jnp.zeros((16, 128), F32)
        return lax.fori_loop(0, LAYERS - 2, step, (zero,) * TRACERS)

    def zero_state():
        elevation = tuple(surface[pl.ds(half * 8, 8), :] for half in range(2))
        flow = tuple(
            tuple(tab[pl.ds((VEL + a) * 16 + half * 8, 8), :] for a in range(2)) for half in range(2)
        )
        return elevation, flow

    def one_round(s, state, work):
        elevation, flow, ghost_flow = state
        centres = [height[pl.ds(half * 8, 8), :] for half in range(2)]
        own_rows = [(j, lambda j=j: wide(height[pl.ds(j, 1), :])) for j in range(16)]
        partial = own_sum(own_rows, centres)
        work()
        pltpu.make_async_copy(far_box.at[s], far_box.at[s], far_recv.at[s]).wait()
        pltpu.make_async_copy(near_box.at[s], near_box.at[s], near_recv.at[s]).wait()

        @pl.when(s == 0)
        def _():
            for b in range(4):
                pltpu.make_async_copy(force_in.at[b], force_in.at[b], force_recv.at[b]).wait()
                for a in range(2):
                    for copy in range(2):
                        row = force_in[b, pl.ds(a * 4 + b, 1), :]
                        ghost_rows[pl.ds(8 + a * 8 + copy * 4 + b, 1), :] = row

        return take_round(s, elevation, flow, ghost_flow, partial)

    elevation, flow = zero_state()
    send_round(0, elevation)
    pltpu.make_async_copy(ghost_fixed, ghost_fixed, fixed_recv).wait()
    by_edge(ghost_fixed, ghost_lane, ghost_block, ghost_g)
    for b in range(4):
        for copy in range(2):
            for row, field in ((0, COR), (24, VEL), (32, VEL + 1)):
                ghost_rows[pl.ds(row + copy * 4 + b, 1), :] = ghost_fixed[pl.ds(b * FIXED + field, 1), :]
    ghost_flow = (ghost_rows[pl.ds(24, 8), :], ghost_rows[pl.ds(32, 8), :])

    def split_halo():
        pltpu.make_async_copy(halo_in, halo_in, halo_recv).wait()
        for b in range(4):
            value = halo_in[b]
            high = value.astype(BF16)
            halo_parts[pl.ds(0, ROWS), pl.ds(b * 128, 128)] = high
            halo_parts[pl.ds(ROWS, ROWS), pl.ds(b * 128, 128)] = (value - high.astype(F32)).astype(BF16)

    def sweep_down(index, carry):
        above = gain_above[layer(index), :]
        share = above * carry[0]
        gain_above[layer(index), :] = share
        out = []
        for t in range(TRACERS):
            rows = layer(t * LAYERS + index)
            value = profile[rows, :] + above * carry[1 + t]
            profile[rows, :] = value
            out.append(value)
        return (share, *out)

    def place_out(c, carry):
        cells = pl.ds(pl.multiple_of(c * 128, 128), 128)
        deep = lax.broadcasted_iota(I32, (8, 128), 0) > 1
        for g in range(ROWS // 8):
            value = profile[pl.ds(g * 128 + c, 8, stride=16), :]
            if g % 8 == 0:
                value = jnp.where(deep, value, 0.0)
            total[pl.ds(g * 8, 8), cells] = value
        for g in range(LAYERS // 8):
            thick[pl.ds(g * 8, 8), cells] = gain_above[pl.ds(g * 128 + c, 8, stride=16), :]
        return carry

    stores = (
        pltpu.make_async_copy(total, rest_hbm, store_sem.at[0]),
        pltpu.make_async_copy(thick, share_hbm, store_sem.at[1]),
    )

    def solve_below():
        values = sweep_up()
        for t in range(TRACERS):
            tops[pl.ds(t * 16, 16), :] = values[t]
        zero, one = jnp.zeros((16, 128), F32), jnp.ones((16, 128), F32)
        gain_above[layer(0), :] = zero
        gain_above[layer(1), :] = one
        lax.fori_loop(2, LAYERS, sweep_down, (one,) + (zero,) * TRACERS)
        lax.fori_loop(0, BLOCKS, place_out, 0)
        for store in stores:
            store.start()

    def tracer_work(s):
        @pl.when(s == 0)
        def _():
            select_halo()

        @pl.when(s < 4)
        def _():
            send_halo(s)

        @pl.when(jnp.logical_and(s >= 1, s < 5))
        def _():
            def step(i, carry):
                mix_own(2 * (s - 1) + i)
                return carry

            lax.fori_loop(0, 2, step, 0)

        @pl.when(s == 5)
        def _():
            split_halo()
            remap(0)

        @pl.when(jnp.logical_and(s >= 5, s < 7))
        def _():
            def step(i, carry):
                mix_halo(4 * (s - 5) + i)
                return carry

            lax.fori_loop(0, 4, step, 0)

        @pl.when(s == 7)
        def _():
            solve_below()

    def subcycle(s, state):
        state = one_round(s, state, lambda: tracer_work(s))

        @pl.when(s < SUBCYCLES - 1)
        def _():
            send_round(s + 1, state[0])

        return state

    elevation, flow, ghost_flow = lax.fori_loop(0, SUBCYCLES, subcycle, (elevation, flow, ghost_flow))

    for half in range(2):
        final_surface[pl.ds(half * 8, 8), :] = elevation[half]
    for c in range(BLOCKS):
        final_velocity[0:1, pl.ds(c * 128, 128)] = speed[pl.ds(c, 1), :]
        final_velocity[1:2, pl.ds(c * 128, 128)] = speed[pl.ds(24 + c, 1), :]

    top = thick_cells[layer(0), :] + jnp.tanh(final_surface[...])
    second = thick_cells[layer(1), :]
    couple_zero = couple(0, top)
    inverse_one = 1.0 / (second + couple_zero + couple_one - couple_one * gain_two)
    gain_one = couple_zero * inverse_one
    inverse_zero = 1.0 / (top + couple_zero - couple_zero * gain_one)
    for t in range(TRACERS):
        rows_zero, rows_one = layer(t * LAYERS), layer(t * LAYERS + 1)
        value_one = (second * profile[rows_one, :] + couple_one * tops[pl.ds(t * 16, 16), :]) * inverse_one
        right = top * profile[rows_zero, :] + FLUX_GAIN * flux[pl.ds(t * 16, 16), :]
        value_zero = (right + couple_zero * value_one) * inverse_zero
        square[pl.ds(t * 16, 16), :] = value_zero
        square[pl.ds(64 + t * 16, 16), :] = value_one + gain_one * value_zero
    for c in range(BLOCKS):
        heads[:, pl.ds(c * 128, 128)] = square[pl.ds(c, 8, stride=16), :]

    for store in stores:
        store.wait()
    pltpu.make_async_copy(near_box, near_box, near_send).wait()
    pltpu.make_async_copy(far_box, far_box, far_send).wait()
    pltpu.make_async_copy(list_fixed, list_fixed, fixed_send).wait()
    pltpu.make_async_copy(force_in, force_in, force_send).wait()
    pltpu.make_async_copy(halo_out, halo_out, halo_send_sem).wait()
    pltpu.make_async_copy(gathered, gathered, col_send).wait()
    pltpu.make_async_copy(arrived.at[others], arrived.at[others], ocn_send).wait()


def finish_kernel(
    rest_hbm, share_hbm, heads_hbm, surface_hbm, flow_hbm, mixed_hbm, surface_out, flow_out,
    rest, share, heads, load_sem, store_sem,
):
    loads = [
        pltpu.make_async_copy(share_hbm, share, load_sem.at[0]),
        pltpu.make_async_copy(heads_hbm, heads, load_sem.at[1]),
    ]
    stores = [
        pltpu.make_async_copy(surface_hbm, surface_out, store_sem.at[0]),
        pltpu.make_async_copy(flow_hbm, flow_out, store_sem.at[1]),
    ]
    pieces = [pl.ds(start, PIECE) for start in range(0, ROWS, PIECE)]
    for i, rows in enumerate(pieces):
        loads.append(pltpu.make_async_copy(rest_hbm.at[rows], rest.at[rows], load_sem.at[2 + i]))
        stores.append(pltpu.make_async_copy(rest.at[rows], mixed_hbm.at[rows], store_sem.at[2 + i]))
    for copy in loads + stores[:2]:
        copy.start()
    loads[0].wait()
    loads[1].wait()
    sub = lax.broadcasted_iota(I32, (8, 2048), 0)
    for i in range(len(pieces)):
        loads[2 + i].wait()
        t = i * PIECE // LAYERS
        head = jnp.broadcast_to(heads[pl.ds(4 + t, 1), :], (8, 2048))
        for first in range(i * PIECE, (i + 1) * PIECE, 8):
            rows = pl.ds(first, 8)
            value = rest[rows, :] + share[pl.ds(first % LAYERS, 8), :] * head
            if first % LAYERS == 0:
                value = jnp.where(sub == 0, jnp.broadcast_to(heads[pl.ds(t, 1), :], (8, 2048)), value)
            rest[rows, :] = value
        stores[2 + i].start()
    for store in stores:
        store.wait()


def finish(*operands):
    hbm = pl.BlockSpec(memory_space=pl.ANY)
    return pl.pallas_call(
        finish_kernel,
        name="finish",
        out_shape=(
            jax.ShapeDtypeStruct((ROWS, 2048), F32),
            jax.ShapeDtypeStruct((16, 128), F32),
            jax.ShapeDtypeStruct((2, 2048), F32),
        ),
        in_specs=[hbm] * 5,
        out_specs=(hbm,) * 3,
        scratch_shapes=[
            pltpu.VMEM((ROWS, 2048), F32),
            pltpu.VMEM((LAYERS, 2048), F32),
            pltpu.VMEM((8, 2048), F32),
            pltpu.SemaphoreType.DMA((2 + ROWS // PIECE,)),
            pltpu.SemaphoreType.DMA((2 + ROWS // PIECE,)),
        ],
        compiler_params=pltpu.CompilerParams(vmem_limit_bytes=60 << 20),
    )(*operands)


def ocean(ocn_size, col_size, *operands):
    vmem = pl.BlockSpec(memory_space=pltpu.VMEM)
    hbm = pl.BlockSpec(memory_space=pl.ANY)

    def kernel(*refs):
        ocean_kernel(ocn_size, col_size, *refs)

    scratch = [
        pltpu.VMEM((8, 2048), F32),
        pltpu.VMEM((16, 128), I32),
        pltpu.VMEM((4, 2048), I32),
        pltpu.VMEM((4, 2048), F32),
        pltpu.VMEM((1, 4, 128), I32),
        pltpu.VMEM((EDGES, 2048), I32),
        pltpu.VMEM((EDGES, 2, 2048), F32),
        pltpu.VMEM((16, 128), F32),
        pltpu.VMEM((16, 128), F32),
        pltpu.VMEM((2, 2048), F32),
        pltpu.VMEM((EDGES, 2048), F32),
        pltpu.VMEM((16, 128), I32),
        pltpu.VMEM((LAYERS, 2048), F32),
        pltpu.VMEM((LAYERS - 1, 2048), F32),
        pltpu.VMEM((ROWS, 2048), F32),
        pltpu.VMEM((FIXED * 16, 128), F32),
        pltpu.VMEM((128, 128), F32),
        pltpu.VMEM((ocn_size // 2, 2 * col_size, 1, 128), F32),
        pltpu.VMEM((2 * col_size, ocn_size // 2, 1, 128), F32),
        pltpu.VMEM((ocn_size * col_size, 1, 128), F32),
        pltpu.VMEM((16, 8, 128), F32),
        pltpu.VMEM((16, 8, 128), F32),
        pltpu.VMEM((128, 128), F32),
        pltpu.VMEM((4 * FIXED, 128), F32),
        pltpu.VMEM((4 * FIXED, 128), F32),
        pltpu.VMEM((8, 128), F32),
        pltpu.VMEM((4, 8, 128), F32),
        pltpu.VMEM((96, 128), I32),
        pltpu.VMEM((96, 128), I32),
        pltpu.VMEM((24, 128), I32),
        pltpu.VMEM((24, 128), I32),
        pltpu.VMEM((48, 128), F32),
        pltpu.VMEM((24, 128), I32),
        pltpu.VMEM((24, 128), I32),
        pltpu.VMEM((48, 128), F32),
        pltpu.VMEM((16, 128), F32),
        pltpu.VMEM((48, 128), F32),
        pltpu.VMEM((40, 128), F32),
        pltpu.VMEM((SUBCYCLES, 4, 8, 128), F32),
        pltpu.VMEM((SUBCYCLES, 4, 8, 128), F32),
        pltpu.VMEM((SUBCYCLES, 4, 8, 128), F32),
        pltpu.VMEM((4, ROWS, 128), F32),
        pltpu.VMEM((4, ROWS, 128), F32),
        pltpu.VMEM((2 * ROWS, 2048), BF16),
        pltpu.VMEM((2 * ROWS, 512), BF16),
        pltpu.VMEM((ROWS, 2048), F32),
        pltpu.VMEM((ROWS * 16, 128), F32),
        pltpu.VMEM((LAYERS * 16, 128), F32),
        pltpu.VMEM((LAYERS * 16, 128), F32),
        pltpu.VMEM((LAYERS * 16, 128), F32),
        pltpu.VMEM((LAYERS * 16, 128), F32),
        pltpu.VMEM((LAYERS * 16, 128), F32),
        pltpu.VMEM((TRACERS * 16, 128), F32),
        pltpu.SemaphoreType.DMA((15,)),
        pltpu.SemaphoreType.DMA((2,)),
        pltpu.SemaphoreType.DMA,
        pltpu.SemaphoreType.DMA,
        pltpu.SemaphoreType.DMA,
        pltpu.SemaphoreType.DMA,
        pltpu.SemaphoreType.DMA,
        pltpu.SemaphoreType.DMA,
        pltpu.SemaphoreType.DMA,
        pltpu.SemaphoreType.DMA,
        pltpu.SemaphoreType.DMA,
        pltpu.SemaphoreType.DMA((4,)),
        pltpu.SemaphoreType.DMA,
        pltpu.SemaphoreType.DMA,
        pltpu.SemaphoreType.DMA,
        pltpu.SemaphoreType.DMA((SUBCYCLES,)),
        pltpu.SemaphoreType.DMA,
        pltpu.SemaphoreType.DMA((SUBCYCLES,)),
    ]
    return pl.pallas_call(
        kernel,
        name="ocean",
        out_shape=(
            jax.ShapeDtypeStruct((ROWS, 2048), F32),
            jax.ShapeDtypeStruct((LAYERS, 2048), F32),
            jax.ShapeDtypeStruct((8, 2048), F32),
            jax.ShapeDtypeStruct((16, 128), F32),
            jax.ShapeDtypeStruct((2, 2048), F32),
        ),
        in_specs=[hbm] * 15,
        out_specs=(hbm, hbm, vmem, vmem, vmem),
        scratch_shapes=scratch,
        compiler_params=pltpu.CompilerParams(
            collective_id=0, has_side_effects=True, vmem_limit_bytes=60 << 20
        ),
    )(*operands)


def solution(mesh):
    ocn_size, col_size = mesh.shape["ocn"], mesh.shape["col"]

    def per_device(
        air_flux,
        send_index,
        remap_column,
        remap_weight,
        halo_send,
        neighbours,
        gradient_weight,
        coriolis,
        sea_surface,
        velocity,
        lateral_weight,
        layer_count,
        thickness,
        diffusivity,
        tracers,
    ):
        solved = ocean(
            ocn_size,
            col_size,
            air_flux,
            send_index[0].T,
            remap_column,
            remap_weight,
            halo_send,
            neighbours,
            jnp.swapaxes(gradient_weight, 0, 1),
            coriolis.reshape(16, 128),
            sea_surface.reshape(16, 128),
            velocity,
            lateral_weight,
            layer_count.reshape(16, 128),
            thickness,
            diffusivity,
            tracers.reshape(ROWS, 2048),
        )
        mixed, elevation, flow = finish(*solved)
        return mixed.reshape(TRACERS, LAYERS, 2048), elevation.reshape(2048), flow

    both = ("ocn", "col")
    placed = (
        P(None, both),
        P(both, None, None),
        P(None, both),
        P(None, both),
        P(both, None, None),
        P(None, both),
        P(None, None, both),
        P(both),
        P(both),
        P(None, both),
        P(None, both),
        P(both),
        P(None, both),
        P(None, both),
        P(None, None, both),
    )
    return jax.shard_map(
        per_device,
        mesh=mesh,
        in_specs=placed,
        out_specs=(P(None, None, both), P(both), P(None, both)),
        check_vma=False,
    )
```
